32 devices in a mesh: req: 4 (over y, x), kv: 4 (over z), blk: 2 (over core).
Axes of the slice: x: 2, y: 2, z: 4, core: 2. Of those that a mesh axis runs over, the one named last changes fastest.
Arguments:
- x_resid: bfloat16 [4, 256, 5120], P('req', ('kv', 'blk')), may hold values from -54 to 54
- q_new: bfloat16 [4, 256, 2048], P('req', None, 'kv'), may hold values from -36 to 36
- k_new: bfloat16 [4, 256, 512], P('req', None, 'kv'), may hold values from -6 to 12
- v_new: bfloat16 [4, 256, 512], P('req', None, 'kv'), may hold values from -24 to 24
- k_cache: bfloat16 [4, 4, 64, 128, 128], P('req', 'kv', 'blk'), may hold values from -6 to 12
- v_cache: bfloat16 [4, 4, 64, 128, 128], P('req', 'kv', 'blk'), may hold values from -24 to 24
- cache_len: int32 [4], P('req'), may hold values from 1 to 7936, as said below
- page_table: int32 [4, 64], P('req'), may hold values from 0 to 63, as said below
- wo: bfloat16 [2048, 5120], P(('kv', 'blk')), may hold values from -0.125 to 0.125
- norm_gain: bfloat16 [5120], replicated, may hold values from 0.099609375 to 1.8984375
- w_gate: bfloat16 [5120, 7168], P('req', ('kv', 'blk')), may hold values from -0.078125 to 0.078125
- w_up: bfloat16 [5120, 7168], P('req', ('kv', 'blk')), may hold values from -0.078125 to 0.078125
- w_down: bfloat16 [7168, 5120], P(('kv', 'blk'), 'req'), may hold values from -0.0625 to 0.0625
Outputs:
- layer_out: bfloat16 [4, 256, 5120], P('req', ('kv', 'blk'))
- k_cache_out: bfloat16 [4, 4, 64, 128, 128], P('req', 'kv', 'blk')
- v_cache_out: bfloat16 [4, 4, 64, 128, 128], P('req', 'kv', 'blk')
The draws below stay inside these ranges and needn't reach their ends.
Inputs may be any that keep to these rules, and one draw needn't show every extreme that they name: `cache_len`: at least one request has the largest length. `page_table`: each row is a permutation of 0 to 63.
All inputs are finite; a program needn't handle non-finite values.
Results may differ from the reference program's by a relative error of at most 0.0095.
Values may be sent and summed in bfloat16 or wider, within the bound.
No kernel may reach another device: no remote copies, remote signals or barrier semaphores. Data moves between devices by JAX's collectives and lax.ppermute only.
A program may use at most 128 MiB of HBM per device.

```python
import math
import jax
import jax.numpy as jnp
from jax import lax

D = 5120
HD = 128
GROUP = 4
FFW = 7168
C = 256
PAGE = 128
SLOTS = 32
KVH = 4
HEADS = 16
NPAGE = 64
REQS = 4
N_BLK = 2


def draw_q_new(key, part):
    first_key = jax.random.fold_in(key, 0)
    base = jnp.clip(jax.random.normal(first_key, (REQS, C, HEADS, HD), jnp.float32), -6.0, 6.0)
    return base.reshape(REQS, C, HEADS * HD).astype(jnp.bfloat16)


def draw_k_new(key, part):
    first_key = jax.random.fold_in(key, 0)
    base = jnp.clip(jax.random.normal(first_key, (REQS, C, KVH, HD), jnp.float32), -6.0, 6.0)
    return base.reshape(REQS, C, KVH * HD).astype(jnp.bfloat16)


def draw_k_cache(key, part):
    first_key = jax.random.fold_in(key, 0)
    base = jnp.clip(jax.random.normal(first_key, (REQS, KVH, NPAGE, PAGE, HD), jnp.float32), -6.0, 6.0)
    return base.astype(jnp.bfloat16)


def draw_x_resid(key, part):
    first_key, second_key, third_key = jax.random.split(key, 3)
    base = jnp.clip(jax.random.normal(first_key, (REQS, C, D), jnp.float32), -6.0, 6.0)
    row_scale = jnp.exp(jax.random.uniform(second_key, (REQS, C, 1), jnp.float32, jnp.log(0.3), jnp.log(3.0)))
    column_scale = jnp.exp(jax.random.uniform(third_key, (D,), jnp.float32, jnp.log(0.3), jnp.log(3.0)))
    return (base * row_scale * column_scale).astype(jnp.bfloat16)


def draw_cache_len(key, part):
    keys_all = jax.random.split(key, 4)
    longest = NPAGE * PAGE - C
    first_draw = jax.random.randint(keys_all[0], (REQS,), 0, longest + 1)
    second_draw = jax.random.randint(keys_all[1], (REQS,), 0, longest + 1)
    third_draw = jax.random.randint(keys_all[2], (REQS,), 0, longest + 1)
    lengths = first_draw * second_draw // longest * third_draw // longest
    lengths = jnp.maximum(lengths, 1)
    picked = jax.random.randint(keys_all[3], (), 0, REQS)
    return jnp.where(jnp.arange(REQS) == picked, longest, lengths).astype(jnp.int32)


def draw_page_table(key, part):
    request_keys = jax.random.split(key, REQS)
    return jax.vmap(lambda single: jax.random.permutation(single, NPAGE))(request_keys).astype(jnp.int32)


def level_of(key, extent, cuts, least, largest):
    gain = 1.0
    for position, shards_of in cuts:
        draws = jax.random.uniform(jax.random.fold_in(jax.random.fold_in(key, 6), position), (shards_of,), jnp.float32, least / len(cuts), largest / len(cuts))
        gain = gain * jnp.repeat(jnp.exp(draws), extent[position] // shards_of).reshape((-1,) + (1,) * (len(extent) - 1 - position))
    return gain


def scatter_about(key, shape, scale, limit, shards=(), kind=jnp.bfloat16):
    array = jax.random.normal(key, shape, jnp.float32) * scale
    if len(shards) > 0:
        array = level_of(key, shape, shards, -0.22, 0.18) * array
    return jnp.clip(array, min=-limit, max=limit).astype(kind)


def setup_inputs(seed: int = 0) -> dict:
    key_of = jax.random.split(jax.random.key(seed), 14)
    return {
        "x_resid": draw_x_resid(jax.random.fold_in(key_of[13], 71), 0),
        "q_new": draw_q_new(jax.random.fold_in(key_of[13], 71), 0),
        "k_new": draw_k_new(jax.random.fold_in(key_of[13], 71), 0),
        "v_new": scatter_about(key_of[3], (REQS, C, KVH * HD), 4.0, 24.0, ((0, 4), (2, 4))),
        "k_cache": draw_k_cache(jax.random.fold_in(key_of[13], 71), 0),
        "v_cache": scatter_about(key_of[5], (REQS, KVH, NPAGE, PAGE, HD), 4.0, 24.0, ((0, 4), (1, 4), (2, 2))),
        "cache_len": draw_cache_len(jax.random.fold_in(key_of[13], 71), 0),
        "page_table": draw_page_table(jax.random.fold_in(key_of[13], 71), 0),
        "wo": scatter_about(key_of[8], (HEADS * HD, D), (HEADS * HD) ** -0.5, 0.125, ((0, 8),)),
        "norm_gain": jnp.clip(1.0 + 0.18 * jax.random.normal(key_of[9], (D,), jnp.float32), 0.099609375, 1.8984375).astype(jnp.bfloat16),
        "w_gate": scatter_about(key_of[10], (D, FFW), D ** -0.5, 0.078125, ((0, 4), (1, 8))),
        "w_up": scatter_about(key_of[11], (D, FFW), D ** -0.5, 0.078125, ((0, 4), (1, 8))),
        "w_down": scatter_about(key_of[12], (FFW, D), FFW ** -0.5, 0.0625, ((0, 8), (1, 4))),
    }


def rotate(field, positions):
    half_width = field.shape[-1] // 2
    pair_index = jnp.arange(half_width, dtype=jnp.float32)
    frequency = jnp.power(1000000.0, -2.0 * pair_index / field.shape[-1])
    angles = positions.astype(jnp.float32)[:, None] * frequency[None, :]
    cosine = jnp.cos(angles)
    sine_part = jnp.sin(angles)
    lower_half = field[..., :half_width]
    upper_half = field[..., half_width:]
    return jnp.concatenate([lower_half * cosine - upper_half * sine_part, upper_half * cosine + lower_half * sine_part], axis=-1)

def attend_head(queries, key_rows, value_rows, key_position, query_position):
    key_blocks = key_rows.reshape(N_BLK, SLOTS * PAGE, HD).astype(jnp.float32)
    value_blocks = value_rows.reshape(N_BLK, SLOTS * PAGE, HD).astype(jnp.float32)
    position_blocks = key_position.reshape(N_BLK, 1, 1, SLOTS * PAGE)
    scores = jnp.einsum('gcd,bsd->bgcs', queries.astype(jnp.float32), key_blocks) * (1.0 / math.sqrt(HD))
    allowed = position_blocks <= query_position[None, None, :, None]
    masked = jnp.where(allowed, scores, -1e+30)
    block_max = lax.optimization_barrier(jnp.max(masked, axis=-1))
    weights = jnp.where(allowed, jnp.exp(masked - block_max[..., None]), 0.0).astype(jnp.bfloat16)
    block_total = lax.optimization_barrier(jnp.sum(weights.astype(jnp.float32), axis=-1))
    block_out = jnp.einsum('bgcs,bsd->bgcd', weights.astype(jnp.float32), value_blocks)
    overall = lax.optimization_barrier(jnp.max(block_max, axis=0))
    factor = jnp.exp(block_max - overall[None])
    total_sum = lax.optimization_barrier(jnp.sum(factor * block_total, axis=0))
    weighted = lax.optimization_barrier(jnp.sum(factor[..., None] * block_out, axis=0))
    return (weighted / total_sum[..., None]).astype(jnp.bfloat16)

def one_request(inputs):
    length, page_rows, queries, new_keys, new_values, key_cache, value_cache = inputs
    positions = length + jnp.arange(C, dtype=jnp.int32)
    query_heads = rotate(queries.reshape(C, HEADS, HD).astype(jnp.float32).transpose(1, 0, 2), positions).astype(jnp.bfloat16)
    key_heads = rotate(new_keys.reshape(C, KVH, HD).astype(jnp.float32).transpose(1, 0, 2), positions).astype(jnp.bfloat16)
    value_heads = new_values.reshape(C, KVH, HD).transpose(1, 0, 2)
    page_ids = jnp.arange(NPAGE, dtype=jnp.int32)
    logical = lax.optimization_barrier(jnp.sum(jnp.where(page_rows[None, :] == page_ids[:, None], page_ids[None, :], 0), axis=1))
    slot_position = (logical[:, None] * PAGE + jnp.arange(PAGE, dtype=jnp.int32)[None, :]).reshape(NPAGE * PAGE)
    new_index = slot_position - length
    is_new = (new_index >= 0) & (new_index < C)
    chosen = jnp.clip(new_index, 0, C - 1)
    key_flat = jnp.where(is_new[None, :, None], key_heads[:, chosen], key_cache.reshape(KVH, NPAGE * PAGE, HD))
    value_flat = jnp.where(is_new[None, :, None], value_heads[:, chosen], value_cache.reshape(KVH, NPAGE * PAGE, HD))
    attn = lax.map(lambda group_in: attend_head(group_in[0], group_in[1], group_in[2], slot_position, positions), (query_heads.reshape(KVH, GROUP, C, HD), key_flat, value_flat))
    attn_rows = attn.reshape(HEADS, C, HD).transpose(1, 0, 2).reshape(C, HEADS * HD)
    return (attn_rows, key_flat.reshape(KVH, NPAGE, PAGE, HD), value_flat.reshape(KVH, NPAGE, PAGE, HD))

def reference(x_resid, q_new, k_new, v_new, k_cache, v_cache, cache_len, page_table, wo, norm_gain, w_gate, w_up, w_down):
    attn, key_out, value_out = lax.map(one_request, (cache_len, page_table, q_new, k_new, v_new, k_cache, v_cache))

    def feed_forward(inputs):
        residual_in, attn_rows = inputs
        resid = residual_in.astype(jnp.float32) + jnp.dot(attn_rows, wo, preferred_element_type=jnp.float32)
        normed = (resid * lax.rsqrt(lax.optimization_barrier(jnp.mean(resid * resid, axis=-1, keepdims=True)) + 1e-05) * norm_gain.astype(jnp.float32)).astype(jnp.bfloat16)
        gate_val = jnp.dot(normed, w_gate, preferred_element_type=jnp.float32)
        up_val = jnp.dot(normed, w_up, preferred_element_type=jnp.float32)
        hidden = (jax.nn.silu(gate_val) * up_val).astype(jnp.bfloat16)
        return (resid + jnp.dot(hidden, w_down, preferred_element_type=jnp.float32)).astype(jnp.bfloat16)
    layer_out = lax.map(feed_forward, (x_resid, attn))
    return (layer_out, key_out, value_out)
```

```python
import functools
import math

import jax
import jax.numpy as jnp
import numpy as np
from jax import lax
from jax.experimental import pallas as pl
from jax.experimental.pallas import tpu as pltpu
from jax.sharding import PartitionSpec as P

NEG = -1e30
F32 = jnp.float32
BF16 = jnp.bfloat16
VMEM = pl.BlockSpec(memory_space=pltpu.VMEM)
SMEM = pl.BlockSpec(memory_space=pltpu.SMEM)


def swap(a, axis, mask):
    return lax.ppermute(a, axis, [(i, i ^ mask) for i in range(lax.axis_size(axis))])


def reduce_bits(x, axis, order, last=F32):
    count = x.shape[0]
    left = list(range(count.bit_length() - 1))[::-1]
    x = x.reshape((2,) * len(left) + x.shape[1:])
    for bit in order:
        dim = left.index(bit)
        left.remove(bit)
        kept = lax.index_in_dim(x, 0, dim, False).astype(F32)
        came = swap(lax.index_in_dim(x, 1, dim, False), axis, 1 << bit).astype(F32)
        x = (kept + came).astype(BF16 if left else last)
    return x


def gather_bits(x, axis):
    x = x[None]
    for bit in range(lax.axis_size(axis).bit_length() - 1)[::-1]:
        came = swap(x, axis, 1 << bit)
        x = jnp.stack([x, came], 1).reshape((2 * x.shape[0],) + x.shape[1:])
    return x


def trade(pieces, axis):
    return [pieces[0]] + [swap(piece, axis, j) for j, piece in enumerate(pieces) if j]


def attention_body(shape, scal, table, freq, q_ref, kn_ref, vn_ref, kc_ref, vc_ref,
                   ko_ref, vo_ref, ok_ref, os_ref, sk_ref, ss_ref,
                   inverse, key_pos, q_rot):
    kv_count, chunks, rows = shape
    tokens, head_dim = kn_ref.shape
    slots, page = kc_ref.shape[0], kc_ref.shape[1]
    heads = q_ref.shape[1] // head_dim
    pages = table.shape[1]
    length, kv_id, blk_id = scal[0], scal[1], scal[2]
    head = pl.program_id(0)
    scale = 1.0 / math.sqrt(head_dim)

    @pl.when(head == 0)
    def _():
        @pl.loop(0, pages)
        def _(j):
            inverse[table[0, j]] = j

        lane = lax.broadcasted_iota(jnp.int32, (1, page), 1)
        for s in range(slots):
            key_pos[:, s * page:(s + 1) * page] = inverse[blk_id * slots + s] * page + lane

        where_at = (length + lax.broadcasted_iota(jnp.int32, (tokens, head_dim), 0)).astype(F32)
        angle = where_at * freq[...]
        cosine = jnp.cos(angle)
        sine = jnp.sin(angle)
        low = lax.broadcasted_iota(jnp.int32, (tokens, head_dim), 1) < head_dim // 2
        sine = jnp.where(low, -sine, sine)

        def rotate(u):
            u = u.astype(F32)
            return (u * cosine + pltpu.roll(u, head_dim // 2, 1) * sine).astype(BF16)

        for h in range(heads):
            cols = slice(h * head_dim, (h + 1) * head_dim)
            q_rot[:, cols] = rotate(q_ref[:, cols])
        k_rot = rotate(kn_ref[...])

        ko_ref[...] = kc_ref[...]
        vo_ref[...] = vc_ref[...]
        for extra in range(tokens // page + 1):
            logical = length // page + extra
            slot = table[0, jnp.minimum(logical, pages - 1)] - blk_id * slots

            @pl.when((logical < pages) & (slot >= 0) & (slot < slots))
            def _():
                first = logical * page - length
                at = first + lax.broadcasted_iota(jnp.int32, (page, tokens), 0)
                pick = (at == lax.broadcasted_iota(jnp.int32, (page, tokens), 1)).astype(BF16)
                fresh_k = jnp.dot(pick, k_rot, preferred_element_type=F32).astype(BF16)
                fresh_v = jnp.dot(pick, vn_ref[...], preferred_element_type=F32).astype(BF16)
                at = first + lax.broadcasted_iota(jnp.int32, (page, head_dim), 0)
                is_new = (at >= 0) & (at < tokens)
                ko_ref[slot] = jnp.where(is_new, fresh_k, ko_ref[slot])
                vo_ref[slot] = jnp.where(is_new, fresh_v, vo_ref[slot])

    half = tokens // 2
    span = chunks * rows
    hcol = pl.ds(pl.multiple_of(head * head_dim, head_dim), head_dim)
    keys = ko_ref[...].reshape(slots * page, head_dim)
    values = vo_ref[...].reshape(slots * page, head_dim)
    for side in range(2):
        parts = []
        for c in range(chunks):
            for m in range(kv_count):
                start = ((kv_id ^ m) * 2 + (blk_id ^ side)) * span + c * rows
                parts.append(q_rot[pl.ds(pl.multiple_of(start, rows), rows), hcol])
        queries = jnp.concatenate(parts, 0)
        row = lax.broadcasted_iota(jnp.int32, (half, 1), 0)
        group = row // rows
        token = (((group % kv_count) ^ kv_id) * 2 + (blk_id ^ side)) * span
        token = token + (group // kv_count) * rows + row % rows
        scores = lax.dot_general(queries, keys, (((1,), (1,)), ((), ())), preferred_element_type=F32)
        masked = jnp.where(key_pos[...] <= length + token, scores, NEG)
        top = jnp.maximum(jnp.max(masked, 1, keepdims=True), 0.1 * NEG)
        weights = jnp.exp2((masked - top) * (scale * math.log2(math.e))).astype(BF16)
        total = jnp.sum(weights.astype(F32), 1, keepdims=True)
        out = jnp.dot(weights, values, preferred_element_type=F32)
        some = total > 0.0
        safe = jnp.where(some, total, 1.0)
        out = (out / safe).astype(BF16)
        log_sum = jnp.where(some, top * scale + jnp.log(safe), NEG)
        out_ref, stat_ref = ((ok_ref, sk_ref), (os_ref, ss_ref))[side]
        out_ref[:, hcol] = out
        lane = lax.broadcasted_iota(jnp.int32, (half, head_dim), 1)
        before = jnp.where(head == 0, 0.0, stat_ref[...])
        stat_ref[...] = jnp.where(lane == head, log_sum, before)


def attention(scal, table, q, k_new, v_new, k_cache, v_cache, kv_count, chunks, rows):
    tokens, head_dim = k_new.shape
    width = q.shape[1]
    heads = width // head_dim
    slots, page = k_cache.shape[0], k_cache.shape[1]
    half = tokens // 2
    pair = np.arange(head_dim) % (head_dim // 2)
    freq = jnp.asarray((1e6 ** (-2.0 * pair / head_dim)).astype(np.float32)[None])
    whole = lambda *s: pl.BlockSpec(s, lambda h: (0,) * len(s))
    cache = whole(slots, page, head_dim)
    return pl.pallas_call(
        functools.partial(attention_body, (kv_count, chunks, rows)),
        grid=(heads,),
        in_specs=[SMEM, SMEM, whole(1, head_dim), whole(tokens, width), whole(tokens, head_dim),
                  whole(tokens, head_dim), cache, cache],
        out_specs=[cache, cache, whole(half, width), whole(half, width),
                   whole(half, head_dim), whole(half, head_dim)],
        out_shape=[
            jax.ShapeDtypeStruct(k_cache.shape, BF16),
            jax.ShapeDtypeStruct(v_cache.shape, BF16),
            jax.ShapeDtypeStruct((half, width), BF16),
            jax.ShapeDtypeStruct((half, width), BF16),
            jax.ShapeDtypeStruct((half, head_dim), F32),
            jax.ShapeDtypeStruct((half, head_dim), F32),
        ],
        scratch_shapes=[
            pltpu.SMEM((table.shape[1],), jnp.int32),
            pltpu.VMEM((1, slots * page), jnp.int32),
            pltpu.VMEM((tokens, width), BF16),
        ],
        compiler_params=pltpu.CompilerParams(vmem_limit_bytes=48 * 2**20),
        name="attention",
    )(scal, table, freq, q, k_new, v_new, k_cache, v_cache)


def project_body(blk_ref, o1, o2, s1, s2, wa, wb, out_ref, attn):
    head_dim = s1.shape[1]
    heads = o1.shape[1] // head_dim
    depth = wa.shape[0]
    blk_id = blk_ref[0]

    @pl.when(pl.program_id(0) == 0)
    def _():
        for h in range(heads):
            cols = slice(h * head_dim, (h + 1) * head_dim)
            first, second = s1[:, h:h + 1], s2[:, h:h + 1]
            top = jnp.maximum(first, second)
            f1, f2 = jnp.exp(first - top), jnp.exp(second - top)
            mixed = f1 * o1[:, cols].astype(F32) + f2 * o2[:, cols].astype(F32)
            attn[:, cols] = (mixed / (f1 + f2)).astype(BF16)

    mine = attn[:, pl.ds(pl.multiple_of(blk_id * depth, depth), depth)]
    other = attn[:, pl.ds(pl.multiple_of((1 - blk_id) * depth, depth), depth)]
    out_ref[...] = (
        jnp.dot(mine, wa[...], preferred_element_type=F32)
        + jnp.dot(other, wb[...], preferred_element_type=F32)
    ).astype(BF16)


def project(blk, o1, o2, s1, s2, wa, wb):
    rows, width = o1.shape
    model = wa.shape[1]
    step = model // 4
    fixed = lambda a: pl.BlockSpec(a.shape, lambda n: (0, 0))
    weight = pl.BlockSpec((wa.shape[0], step), lambda n: (0, n))
    return pl.pallas_call(
        project_body,
        grid=(model // step,),
        in_specs=[SMEM, fixed(o1), fixed(o2), fixed(s1), fixed(s2), weight, weight],
        out_specs=pl.BlockSpec((rows, step), lambda n: (0, n)),
        out_shape=jax.ShapeDtypeStruct((rows, model), BF16),
        scratch_shapes=[pltpu.VMEM((rows, width), BF16)],
        compiler_params=pltpu.CompilerParams(vmem_limit_bytes=32 * 2**20),
        name="project",
    )(blk, o1, o2, s1, s2, wa, wb)


def on_device(x_resid, q_new, k_new, v_new, k_cache, v_cache, cache_len, page_table,
              wo, norm_gain, w_gate, w_up, w_down):
    reqs, kvs = lax.axis_size("req"), lax.axis_size("kv")
    req_bits = reqs.bit_length() - 1
    kv_bits = kvs.bit_length() - 1
    req_id = lax.axis_index("req")
    blk_id = lax.axis_index("blk")
    span, model = x_resid.shape[1:]
    part = model // reqs
    rows = 16
    chunks = span // rows
    scal = jnp.stack([cache_len[0], lax.axis_index("kv"), blk_id]).astype(jnp.int32)
    blk = blk_id.astype(jnp.int32)[None]

    wo_far, gate_far, up_far, down_far = (swap(w, "blk", 1) for w in (wo, w_gate, w_up, w_down))
    keys_out, values_out, o_keep, o_send, s_keep, s_send = attention(
        scal, page_table, q_new[0], k_new[0], v_new[0], k_cache[0, 0], v_cache[0, 0],
        kvs, chunks, rows)
    o_came, s_came = swap(o_send, "blk", 1), swap(s_send, "blk", 1)

    gain = norm_gain.astype(F32)
    a_order = list(range(req_bits))
    b_order = a_order[req_bits // 2:] + a_order[:req_bits // 2]
    outs = []
    chunk_rows = kvs * rows
    partial_all = project(blk, o_keep, o_came, s_keep, s_came, wo, wo_far)
    for c in range(chunks):
        partial = partial_all[c * chunk_rows:(c + 1) * chunk_rows].reshape(kvs, rows, model)
        summed = reduce_bits(partial, "kv", range(kv_bits))
        resid = x_resid[0, c * rows:(c + 1) * rows].astype(F32) + summed
        normed = (
            resid * lax.rsqrt(jnp.mean(resid * resid, axis=-1, keepdims=True) + 1e-05) * gain
        ).astype(BF16)
        cut = normed.reshape(rows, reqs, part)
        pieces = [lax.dynamic_index_in_dim(cut, req_id ^ j, 1, False) for j in range(reqs)]
        fed = jnp.stack(trade(pieces, "req"))
        fed = gather_bits(fed, "kv")
        flat = fed.reshape(kvs * reqs * rows, part)

        def hidden_of(gate_w, up_w, order):
            both = jnp.concatenate(
                [jnp.dot(flat, w, preferred_element_type=F32).astype(BF16) for w in (gate_w, up_w)], 1)
            both = both.reshape(kvs, reqs, rows, -1).transpose(1, 0, 2, 3)
            both = reduce_bits(both, "req", order)
            gate, up = jnp.split(both, 2, -1)
            return (jax.nn.silu(gate) * up).astype(BF16)

        near = hidden_of(w_gate, w_up, a_order)
        far = hidden_of(gate_far, up_far, b_order)
        near = jnp.stack(trade([near] * reqs, "req"))
        far = jnp.stack(trade([far] * reqs, "req"))
        down = (
            jnp.dot(near.reshape(reqs * kvs * rows, -1), w_down, preferred_element_type=F32)
            + jnp.dot(far.reshape(reqs * kvs * rows, -1), down_far, preferred_element_type=F32)
        ).astype(BF16)
        down = down.reshape(reqs, kvs, rows, part).transpose(1, 0, 2, 3)
        down = reduce_bits(down, "kv", range(kv_bits), BF16)
        came = jnp.stack(trade([down[j] for j in range(reqs)], "req"))
        mlp = [lax.dynamic_index_in_dim(came, req_id ^ j, 0, False) for j in range(reqs)]
        outs.append((resid + jnp.concatenate(mlp, 1).astype(F32)).astype(BF16))
    layer_out = jnp.concatenate(outs, 0)[None]
    return layer_out, keys_out[None, None], values_out[None, None]


def solution(mesh):
    in_specs = (
        P("req", ("kv", "blk"), None),
        P("req", None, "kv"),
        P("req", None, "kv"),
        P("req", None, "kv"),
        P("req", "kv", "blk", None, None),
        P("req", "kv", "blk", None, None),
        P("req"),
        P("req", None),
        P(("kv", "blk"), None),
        P(),
        P("req", ("kv", "blk")),
        P("req", ("kv", "blk")),
        P(("kv", "blk"), "req"),
    )
    out_specs = (
        P("req", ("kv", "blk"), None),
        P("req", "kv", "blk", None, None),
        P("req", "kv", "blk", None, None),
    )
    return jax.shard_map(
        on_device, mesh=mesh, in_specs=in_specs, out_specs=out_specs, check_vma=False
    )
```

```python
import functools
import math

import jax
import jax.numpy as jnp
import numpy as np
from jax import lax
from jax.experimental import pallas as pl
from jax.experimental.pallas import tpu as pltpu
from jax.sharding import PartitionSpec as P

NEG = -1e30
F32 = jnp.float32
BF16 = jnp.bfloat16
VMEM = pl.BlockSpec(memory_space=pltpu.VMEM)
SMEM = pl.BlockSpec(memory_space=pltpu.SMEM)


def swap(a, axis, mask):
    return lax.ppermute(a, axis, [(i, i ^ mask) for i in range(lax.axis_size(axis))])


def reduce_bits(x, axis, order, last=F32):
    first = None
    count = x.shape[0]
    left = list(range(count.bit_length() - 1))[::-1]
    x = x.reshape((2,) * len(left) + x.shape[1:])
    for bit in order:
        dim = left.index(bit)
        left.remove(bit)
        kept = lax.index_in_dim(x, 0, dim, False).astype(F32)
        came = swap(lax.index_in_dim(x, 1, dim, False), axis, 1 << bit)
        if first is None:
            first = came
        x = (kept + came.astype(F32)).astype(BF16 if left else last)
    return x, first


def gather_bits(x, axis):
    x = x[None]
    for bit in range(lax.axis_size(axis).bit_length() - 1)[::-1]:
        came = swap(x, axis, 1 << bit)
        x = jnp.stack([x, came], 1).reshape((2 * x.shape[0],) + x.shape[1:])
    return x


def trade(pieces, axis):
    return [pieces[0]] + [swap(piece, axis, j) for j, piece in enumerate(pieces) if j]


def attention_body(shape, first, *refs):
    kv_count, rows, chunk, span = shape
    if first:
        (scal, table, freq, q_ref, kn_ref, vn_ref, kc_ref, vc_ref,
         ko_ref, vo_ref, q_rot, key_pos, ok_ref, os_ref, sk_ref, ss_ref, inverse) = refs
        tokens, head_dim = kn_ref.shape
        pages = table.shape[1]
    else:
        scal, ko_ref, vo_ref, q_rot, key_pos, ok_ref, os_ref, sk_ref, ss_ref = refs
        tokens, head_dim = q_rot.shape[0], ko_ref.shape[2]
    slots, page = ko_ref.shape[0], ko_ref.shape[1]
    heads = q_rot.shape[1] // head_dim
    length, kv_id, blk_id = scal[0], scal[1], scal[2]
    scale = 1.0 / math.sqrt(head_dim)

    if first:
        @pl.loop(0, pages)
        def _(j):
            inverse[table[0, j]] = j

        lane = lax.broadcasted_iota(jnp.int32, (1, page), 1)
        for s in range(slots):
            key_pos[:, s * page:(s + 1) * page] = inverse[blk_id * slots + s] * page + lane

        where_at = (length + lax.broadcasted_iota(jnp.int32, (tokens, head_dim), 0)).astype(F32)
        angle = where_at * freq[...]
        cosine = jnp.cos(angle)
        sine = jnp.sin(angle)
        low = lax.broadcasted_iota(jnp.int32, (tokens, head_dim), 1) < head_dim // 2
        sine = jnp.where(low, -sine, sine)

        def rotate(u):
            u = u.astype(F32)
            return (u * cosine + pltpu.roll(u, head_dim // 2, 1) * sine).astype(BF16)

        for h in range(heads):
            cols = slice(h * head_dim, (h + 1) * head_dim)
            q_rot[:, cols] = rotate(q_ref[:, cols])
        k_rot = rotate(kn_ref[...])

        ko_ref[...] = kc_ref[...]
        vo_ref[...] = vc_ref[...]
        for extra in range(tokens // page + 1):
            logical = length // page + extra
            slot = table[0, jnp.minimum(logical, pages - 1)] - blk_id * slots

            @pl.when((logical < pages) & (slot >= 0) & (slot < slots))
            def _():
                begin = logical * page - length
                at = begin + lax.broadcasted_iota(jnp.int32, (page, tokens), 0)
                pick = (at == lax.broadcasted_iota(jnp.int32, (page, tokens), 1)).astype(BF16)
                fresh_k = jnp.dot(pick, k_rot, preferred_element_type=F32).astype(BF16)
                fresh_v = jnp.dot(pick, vn_ref[...], preferred_element_type=F32).astype(BF16)
                at = begin + lax.broadcasted_iota(jnp.int32, (page, head_dim), 0)
                is_new = (at >= 0) & (at < tokens)
                ko_ref[slot] = jnp.where(is_new, fresh_k, ko_ref[slot])
                vo_ref[slot] = jnp.where(is_new, fresh_v, vo_ref[slot])

    keys = ko_ref[...].reshape(slots * page, head_dim)
    values = vo_ref[...].reshape(slots * page, head_dim)
    side_rows = kv_count * rows
    head_rows = 2 * side_rows
    together = 2
    row = lax.broadcasted_iota(jnp.int32, (together * head_rows, 1), 0) % head_rows
    side = row // side_rows
    group = (row % side_rows) // rows
    token = ((group ^ kv_id) * 2 + (blk_id ^ side)) * span + chunk * rows + row % rows
    lane = lax.broadcasted_iota(jnp.int32, (side_rows, head_dim), 1)
    stats = [jnp.zeros((side_rows, head_dim), F32)] * 2
    for pair in range(heads // together):
        parts = []
        for h in range(pair * together, (pair + 1) * together):
            cols = slice(h * head_dim, (h + 1) * head_dim)
            for s in range(2):
                for m in range(kv_count):
                    start = ((kv_id ^ m) * 2 + (blk_id ^ s)) * span + chunk * rows
                    parts.append(q_rot[pl.ds(pl.multiple_of(start, rows), rows), cols])
        queries = jnp.concatenate(parts, 0)
        scores = lax.dot_general(queries, keys, (((1,), (1,)), ((), ())), preferred_element_type=F32)
        masked = jnp.where(key_pos[...] <= length + token, scores, NEG)
        top = jnp.maximum(jnp.max(masked, 1, keepdims=True), 0.1 * NEG)
        weights = jnp.exp2((masked - top) * (scale * math.log2(math.e))).astype(BF16)
        total = jnp.sum(weights.astype(F32), 1, keepdims=True)
        out = jnp.dot(weights, values, preferred_element_type=F32)
        some = total > 0.0
        safe = jnp.where(some, total, 1.0)
        out = (out / safe).astype(BF16)
        log_sum = jnp.where(some, top * scale + jnp.log(safe), NEG)
        for i in range(together):
            h = pair * together + i
            cols = slice(h * head_dim, (h + 1) * head_dim)
            for s, out_ref in enumerate((ok_ref, os_ref)):
                at = i * head_rows + s * side_rows
                out_ref[:, cols] = out[at:at + side_rows]
                stats[s] = jnp.where(lane == h, log_sum[at:at + side_rows], stats[s])
    sk_ref[...] = stats[0]
    ss_ref[...] = stats[1]


def attend_first(scal, table, q, k_new, v_new, k_cache, v_cache, kv_count, rows, span):
    tokens, head_dim = k_new.shape
    width = q.shape[1]
    slots, page = k_cache.shape[0], k_cache.shape[1]
    side = kv_count * rows
    pair = np.arange(head_dim) % (head_dim // 2)
    freq = jnp.asarray((1e6 ** (-2.0 * pair / head_dim)).astype(np.float32)[None])
    return pl.pallas_call(
        functools.partial(attention_body, (kv_count, rows, 0, span), True),
        in_specs=[SMEM, SMEM] + [VMEM] * 6,
        out_specs=[VMEM] * 8,
        out_shape=[
            jax.ShapeDtypeStruct(k_cache.shape, BF16),
            jax.ShapeDtypeStruct(v_cache.shape, BF16),
            jax.ShapeDtypeStruct((tokens, width), BF16),
            jax.ShapeDtypeStruct((1, slots * page), jnp.int32),
            jax.ShapeDtypeStruct((side, width), BF16),
            jax.ShapeDtypeStruct((side, width), BF16),
            jax.ShapeDtypeStruct((side, head_dim), F32),
            jax.ShapeDtypeStruct((side, head_dim), F32),
        ],
        scratch_shapes=[pltpu.SMEM((table.shape[1],), jnp.int32)],
        compiler_params=pltpu.CompilerParams(vmem_limit_bytes=60 * 2**20),
        name="attend_first",
    )(scal, table, freq, q, k_new, v_new, k_cache, v_cache)


def attend_next(scal, keys, values, q_rot, key_pos, kv_count, rows, chunk, span):
    width, head_dim = q_rot.shape[1], keys.shape[2]
    side = kv_count * rows
    return pl.pallas_call(
        functools.partial(attention_body, (kv_count, rows, chunk, span), False),
        in_specs=[SMEM] + [VMEM] * 4,
        out_specs=[VMEM] * 4,
        out_shape=[
            jax.ShapeDtypeStruct((side, width), BF16),
            jax.ShapeDtypeStruct((side, width), BF16),
            jax.ShapeDtypeStruct((side, head_dim), F32),
            jax.ShapeDtypeStruct((side, head_dim), F32),
        ],
        compiler_params=pltpu.CompilerParams(vmem_limit_bytes=40 * 2**20),
        name="attend_next",
    )(scal, keys, values, q_rot, key_pos)


def project_body(blk_ref, o1, o2, s1, s2, wa, wb, out_ref, attn):
    head_dim = s1.shape[1]
    heads = o1.shape[1] // head_dim
    depth = wa.shape[0]
    blk_id = blk_ref[0]

    @pl.when(pl.program_id(0) == 0)
    def _():
        for h in range(heads):
            cols = slice(h * head_dim, (h + 1) * head_dim)
            first, second = s1[:, h:h + 1], s2[:, h:h + 1]
            top = jnp.maximum(first, second)
            f1, f2 = jnp.exp(first - top), jnp.exp(second - top)
            mixed = f1 * o1[:, cols].astype(F32) + f2 * o2[:, cols].astype(F32)
            attn[:, cols] = (mixed / (f1 + f2)).astype(BF16)

    mine = attn[:, pl.ds(pl.multiple_of(blk_id * depth, depth), depth)]
    other = attn[:, pl.ds(pl.multiple_of((1 - blk_id) * depth, depth), depth)]
    out_ref[...] = (
        jnp.dot(mine, wa[...], preferred_element_type=F32)
        + jnp.dot(other, wb[...], preferred_element_type=F32)
    ).astype(BF16)


def project(blk, o1, o2, s1, s2, wa, wb):
    rows, width = o1.shape
    model = wa.shape[1]
    step = model // 4
    fixed = lambda a: pl.BlockSpec(a.shape, lambda n: (0, 0))
    weight = pl.BlockSpec((wa.shape[0], step), lambda n: (0, n))
    return pl.pallas_call(
        project_body,
        grid=(model // step,),
        in_specs=[SMEM, fixed(o1), fixed(o2), fixed(s1), fixed(s2), weight, weight],
        out_specs=pl.BlockSpec((rows, step), lambda n: (0, n)),
        out_shape=jax.ShapeDtypeStruct((rows, model), BF16),
        scratch_shapes=[pltpu.VMEM((rows, width), BF16)],
        compiler_params=pltpu.CompilerParams(vmem_limit_bytes=32 * 2**20),
        name="project",
    )(blk, o1, o2, s1, s2, wa, wb)


def norm_body(row0, req_ref, x_ref, kept, came, gain_ref, resid_ref, *rest):
    pieces, held = rest[:-1], rest[-1]
    part = pieces[0].shape[1]
    rows = resid_ref.shape[0]
    resid = x_ref[row0:row0 + rows].astype(F32) + (kept[...].astype(F32) + came[...].astype(F32))
    resid_ref[...] = resid
    scale = lax.rsqrt(jnp.mean(resid * resid, axis=-1, keepdims=True) + 1e-05)
    held[...] = (resid * scale * gain_ref[...].astype(F32)).astype(BF16)
    for j, piece in enumerate(pieces):
        start = pl.multiple_of((req_ref[0] ^ j) * part, part)
        piece[...] = held[:, pl.ds(start, part)]


def norm_cut(req, x, kept, came, gain, reqs, row0):
    rows, model = kept.shape
    part = model // reqs
    if part % 128:
        resid = x[row0:row0 + rows].astype(F32) + kept.astype(F32) + came.astype(F32)
        scale = lax.rsqrt(jnp.mean(resid * resid, axis=-1, keepdims=True) + 1e-05)
        cut = (resid * scale * gain.astype(F32)).astype(BF16).reshape(rows, reqs, part)
        return resid, [lax.dynamic_index_in_dim(cut, req[0] ^ j, 1, False) for j in range(reqs)]
    resid, *pieces = pl.pallas_call(
        functools.partial(norm_body, row0),
        in_specs=[SMEM] + [VMEM] * 4,
        out_specs=[VMEM] * (reqs + 1),
        out_shape=[jax.ShapeDtypeStruct((rows, model), F32)]
        + [jax.ShapeDtypeStruct((rows, part), BF16)] * reqs,
        scratch_shapes=[pltpu.VMEM((rows, model), BF16)],
        compiler_params=pltpu.CompilerParams(vmem_limit_bytes=8 * 2**20),
        name="norm_cut",
    )(req, x, kept, came, gain)
    return resid, pieces


def finish_body(req_ref, *refs):
    out_ref = refs[-1]
    at = 0
    chunks = out_ref.shape[0] // refs[0].shape[0]
    count = (len(refs) - 1) // chunks - 1
    for c in range(chunks):
        resid, pieces = refs[at], refs[at + 1:at + 1 + count]
        at += 1 + count
        rows = resid.shape[0]
        for j, piece in enumerate(pieces):
            part = piece.shape[1]
            cols = pl.ds(pl.multiple_of((req_ref[0] ^ j) * part, part), part)
            out_ref[c * rows:(c + 1) * rows, cols] = (
                resid[:, cols] + piece[...].astype(F32)
            ).astype(BF16)


def finish(req, parts):
    part = parts[0][1][0].shape[1]
    if part % 128:
        outs = []
        for resid, pieces in parts:
            came = jnp.stack(pieces)
            mlp = [lax.dynamic_index_in_dim(came, req[0] ^ j, 0, False) for j in range(len(pieces))]
            outs.append((resid + jnp.concatenate(mlp, 1).astype(F32)).astype(BF16))
        return jnp.concatenate(outs, 0)
    flat = [a for resid, pieces in parts for a in [resid] + list(pieces)]
    rows, model = parts[0][0].shape
    return pl.pallas_call(
        finish_body,
        in_specs=[SMEM] + [VMEM] * len(flat),
        out_specs=VMEM,
        out_shape=jax.ShapeDtypeStruct((len(parts) * rows, model), BF16),
        compiler_params=pltpu.CompilerParams(vmem_limit_bytes=8 * 2**20),
        name="finish",
    )(req, *flat)


def after(a, *others):
    return lax.optimization_barrier((a,) + others)[0]


def on_device(x_resid, q_new, k_new, v_new, k_cache, v_cache, cache_len, page_table,
              wo, norm_gain, w_gate, w_up, w_down):
    reqs, kvs = lax.axis_size("req"), lax.axis_size("kv")
    req_bits = reqs.bit_length() - 1
    kv_bits = kvs.bit_length() - 1
    req_id = lax.axis_index("req").astype(jnp.int32)
    blk_id = lax.axis_index("blk").astype(jnp.int32)
    span, model = x_resid.shape[1:]
    part = model // reqs
    rows = 16
    chunks = span // rows
    scal = jnp.stack([cache_len[0], lax.axis_index("kv"), blk_id]).astype(jnp.int32)
    blk, req = blk_id[None], req_id[None]
    near_masks = [0]
    far_masks = list(range(reqs))

    wo_far, gate_far, up_far = (swap(w, "blk", 1) for w in (wo, w_gate, w_up))
    early, late = [], []
    if len(near_masks) > 1:
        quarter = w_down.shape[0] // 4
        late = [w_down[i * quarter:(i + 1) * quarter] for i in range(4)]
        early = [swap(late.pop(0), "req", 1) for _ in range(3)]

    keys_out, values_out, q_rot, key_pos, *got = attend_first(
        scal, page_table, q_new[0], k_new[0], v_new[0], k_cache[0, 0], v_cache[0, 0],
        kvs, rows, span)
    attended = [got] + [
        attend_next(scal, keys_out, values_out, after(q_rot, *early[:1]), key_pos, kvs, rows, c, span)
        for c in range(1, chunks)
    ]
    a_order = list(range(req_bits))
    b_order = a_order[req_bits // 2:] + a_order[:req_bits // 2]

    kept, came = [], []
    last = None
    for o_keep, o_send, s_keep, s_send in attended:
        o_came, s_came = swap(o_send, "blk", 1), swap(s_send, "blk", 1)
        x = project(blk, o_keep, o_came, s_keep, s_came, wo, wo_far).reshape(kvs, rows, model)
        if last is not None:
            x = after(x, last, *early[1:2])
        for bit in range(kv_bits):
            x = x.reshape((-1, 2) + x.shape[1:])
            moved = swap(x[:, 1], "kv", 1 << bit)
            if bit == 0:
                last = moved
            if bit < kv_bits - 1:
                x = (x[:, 0].astype(F32) + moved.astype(F32)).astype(BF16)
        kept.append(x[0, 0])
        came.append(moved[0])

    resids, fed = [], []
    last = None
    for c in range(chunks):
        ready = after(kept[c], *early[2:]) if c == 0 else kept[c]
        resid, pieces = norm_cut(req, x_resid[0], ready, came[c], norm_gain[None], reqs, c * rows)
        resids.append(resid)
        got = jnp.stack(trade(pieces, "req"))
        if c == chunks - 1:
            late = [swap(after(w, got), "req", 1) for w in late]
        if last is not None:
            got = after(got, last)
        x = got[None]
        for bit in range(kv_bits)[::-1]:
            moved = swap(x, "kv", 1 << bit)
            if bit == kv_bits - 1:
                last = moved
            x = jnp.stack([x, moved], 1).reshape((2 * x.shape[0],) + x.shape[1:])
        fed.append(x.reshape(kvs * reqs * rows, part))

    downs = [w_down] + ([jnp.concatenate(early + late)] if early else [])
    downs = [(w, swap(w, "blk", 1)) for w in downs]
    parts = []
    last = None
    for c in range(chunks):
        flat = fed[c]

        def partials(gate_w, up_w):
            both = jnp.concatenate(
                [jnp.dot(flat, w, preferred_element_type=F32).astype(BF16) for w in (gate_w, up_w)], 1)
            return both.reshape(kvs, reqs, rows, -1).transpose(1, 0, 2, 3)

        def hidden_of(both):
            gate, up = jnp.split(both, 2, -1)
            return (jax.nn.silu(gate) * up).astype(BF16)

        near, far = partials(w_gate, w_up), partials(gate_far, up_far)
        if last is not None:
            near, far = after(near, *last), after(far, *last)
        near, near_first = reduce_bits(near, "req", a_order)
        far, far_first = reduce_bits(far, "req", b_order)
        last = near_first, far_first
        near, far = hidden_of(near), hidden_of(far)
        hidden = jnp.concatenate([near, far], -1)
        every = jnp.stack([swap(hidden, "req", h) if h else hidden for h in far_masks])
        every = every.reshape(len(far_masks) * kvs * rows, -1)
        depth = w_down.shape[0]
        down = jnp.stack([
            (
                jnp.dot(every[:, :depth], w, preferred_element_type=F32)
                + jnp.dot(every[:, depth:], w_far, preferred_element_type=F32)
            ).astype(BF16).reshape(len(far_masks), kvs, rows, part).transpose(1, 0, 2, 3)
            for w, w_far in downs
        ], 1)
        down, _ = reduce_bits(down, "kv", range(kv_bits), BF16)
        final = [None] * reqs
        for i, h in enumerate(far_masks):
            block = down[:, i]
            block = swap(block, "req", h) if h else block
            for k, g in enumerate(near_masks):
                final[h ^ g] = block[k]
        parts.append((resids[c], final))
    layer_out = finish(req, parts)[None]
    return layer_out, keys_out[None, None], values_out[None, None]


def solution(mesh):
    in_specs = (
        P("req", ("kv", "blk"), None),
        P("req", None, "kv"),
        P("req", None, "kv"),
        P("req", None, "kv"),
        P("req", "kv", "blk", None, None),
        P("req", "kv", "blk", None, None),
        P("req"),
        P("req", None),
        P(("kv", "blk"), None),
        P(),
        P("req", ("kv", "blk")),
        P("req", ("kv", "blk")),
        P(("kv", "blk"), "req"),
    )
    out_specs = (
        P("req", ("kv", "blk"), None),
        P("req", "kv", "blk", None, None),
        P("req", "kv", "blk", None, None),
    )
    return jax.shard_map(
        on_device, mesh=mesh, in_specs=in_specs, out_specs=out_specs, check_vma=False
    )
```

```python
import functools
import math

import jax
import jax.numpy as jnp
import numpy as np
from jax import lax
from jax.experimental import pallas as pl
from jax.experimental.pallas import tpu as pltpu
from jax.sharding import PartitionSpec as P

NEG = -1e30
F32 = jnp.float32
BF16 = jnp.bfloat16
VMEM = pl.BlockSpec(memory_space=pltpu.VMEM)
SMEM = pl.BlockSpec(memory_space=pltpu.SMEM)
HBM = pl.BlockSpec(memory_space=pltpu.HBM)


def staged(body, scalars, arrays, late, out_shape, scratch, limit, name, out_specs=None):
    count = len(arrays)

    def kernel(*refs):
        n = len(scalars)
        sources, refs_out = refs[n:n + count], refs[n + count:n + count + len(out_shape)]
        rest = refs[n + count + len(out_shape):]
        held, sems, extra = rest[:count], rest[count], rest[count + 1:]
        copies = [
            pltpu.make_async_copy(src, dst, sems.at[i])
            for i, (src, dst) in enumerate(zip(sources, held))
        ]
        for copy in copies:
            copy.start()
        for copy in copies[:count - late]:
            copy.wait()
        waits = [lambda copy=copy: copy.wait() for copy in copies[count - late:]]
        body(*refs[:n], *held, *waits, *refs_out, *extra)

    return pl.pallas_call(
        kernel,
        in_specs=[SMEM] * len(scalars) + [HBM] * count,
        out_specs=out_specs or [VMEM] * len(out_shape),
        out_shape=out_shape,
        scratch_shapes=[pltpu.VMEM(a.shape, a.dtype) for a in arrays]
        + [pltpu.SemaphoreType.DMA((count,))] + list(scratch),
        compiler_params=pltpu.CompilerParams(vmem_limit_bytes=limit * 2**20),
        name=name,
    )(*scalars, *arrays)


def swap(a, axis, mask):
    return lax.ppermute(a, axis, [(i, i ^ mask) for i in range(lax.axis_size(axis))])


def reduce_bits(x, axis, order, last=F32):
    first = None
    count = x.shape[0]
    left = list(range(count.bit_length() - 1))[::-1]
    x = x.reshape((2,) * len(left) + x.shape[1:])
    for bit in order:
        dim = left.index(bit)
        left.remove(bit)
        kept = lax.index_in_dim(x, 0, dim, False).astype(F32)
        came = swap(lax.index_in_dim(x, 1, dim, False), axis, 1 << bit)
        x = (kept + came.astype(F32)).astype(BF16 if left else last)
        first = x if first is None else first
    return x, first


def gather_bits(x, axis):
    x = x[None]
    for bit in range(lax.axis_size(axis).bit_length() - 1)[::-1]:
        came = swap(x, axis, 1 << bit)
        x = jnp.stack([x, came], 1).reshape((2 * x.shape[0],) + x.shape[1:])
    return x


def bind(joint, *values):
    return lax.optimization_barrier(values) if joint else values


def trade(pieces, axis, joint=False):
    return [pieces[0], *bind(joint, *(swap(piece, axis, j) for j, piece in enumerate(pieces) if j))]


def reduce_both_ways(nears, fars, axis):
    sums_near, sums_far = [], []
    for near, far in zip(nears, fars):
        came = bind(True, swap(near[1::2], axis, 1), swap(far[2:], axis, 2), *sums_near, *sums_far)
        sums_near.append((near[::2].astype(F32) + came[0].astype(F32)).astype(BF16))
        sums_far.append((far[:2].astype(F32) + came[1].astype(F32)).astype(BF16))
    near, far = jnp.concatenate(sums_near, 1), jnp.concatenate(sums_far, 1)
    more = bind(True, swap(near[1], axis, 2), swap(far[1], axis, 1))
    return near[0].astype(F32) + more[0].astype(F32), far[0].astype(F32) + more[1].astype(F32)


def attention_body(shape, first, *refs):
    first_m, count, rows, together = shape
    if first:
        (scal, table, freq, q_ref, kn_ref, vn_ref, ko_ref, vo_ref, wait_k, wait_v,
         k_out, v_out, q_rot, key_pos, ok_ref, os_ref, inverse, out_sems) = refs
        tokens, head_dim = kn_ref.shape
        pages = table.shape[1]
    else:
        scal, ko_ref, vo_ref, q_rot, key_pos, ok_ref, os_ref = refs
        tokens, head_dim = q_rot.shape[0], ko_ref.shape[2]
    slots, page = ko_ref.shape[0], ko_ref.shape[1]
    heads = q_rot.shape[1] // head_dim
    length, kv_id, blk_id = scal[0], scal[1], scal[2]
    scale = 1.0 / math.sqrt(head_dim)

    if first:
        @pl.loop(0, pages)
        def _(j):
            inverse[table[0, j]] = j

        lane = lax.broadcasted_iota(jnp.int32, (1, page), 1)
        for s in range(slots):
            key_pos[:, s * page:(s + 1) * page] = inverse[blk_id * slots + s] * page + lane

        where_at = (length + lax.broadcasted_iota(jnp.int32, (tokens, head_dim), 0)).astype(F32)
        angle = where_at * freq[...]
        cosine = jnp.cos(angle)
        sine = jnp.sin(angle)
        low = lax.broadcasted_iota(jnp.int32, (tokens, head_dim), 1) < head_dim // 2
        sine = jnp.where(low, -sine, sine)

        def rotate(u):
            u = u.astype(F32)
            return (u * cosine + pltpu.roll(u, head_dim // 2, 1) * sine).astype(BF16)

        for h in range(heads):
            cols = slice(h * head_dim, (h + 1) * head_dim)
            q_rot[:, cols] = rotate(q_ref[:, cols])
        k_rot = rotate(kn_ref[...])

        wait_k()
        wait_v()
        for extra in range(tokens // page + 1):
            logical = length // page + extra
            slot = table[0, jnp.minimum(logical, pages - 1)] - blk_id * slots

            @pl.when((logical < pages) & (slot >= 0) & (slot < slots))
            def _():
                begin = logical * page - length
                at = begin + lax.broadcasted_iota(jnp.int32, (page, tokens), 0)
                pick = (at == lax.broadcasted_iota(jnp.int32, (page, tokens), 1)).astype(BF16)
                fresh_k = jnp.dot(pick, k_rot, preferred_element_type=F32).astype(BF16)
                fresh_v = jnp.dot(pick, vn_ref[...], preferred_element_type=F32).astype(BF16)
                at = begin + lax.broadcasted_iota(jnp.int32, (page, head_dim), 0)
                is_new = (at >= 0) & (at < tokens)
                ko_ref[slot] = jnp.where(is_new, fresh_k, ko_ref[slot])
                vo_ref[slot] = jnp.where(is_new, fresh_v, vo_ref[slot])

        stores = [
            pltpu.make_async_copy(src, dst, out_sems.at[i])
            for i, (src, dst) in enumerate(((ko_ref, k_out), (vo_ref, v_out)))
        ]
        for store in stores:
            store.start()

    keys = ko_ref[...].reshape(slots * page, head_dim)
    values = vo_ref[...].reshape(slots * page, head_dim)
    side_rows = count * rows
    head_rows = 2 * side_rows
    row = lax.broadcasted_iota(jnp.int32, (together * head_rows, 1), 0) % head_rows
    side = row // side_rows
    place = (row % side_rows) // rows + first_m
    token = ((place ^ kv_id) * 2 + (blk_id ^ side)) * rows + row % rows
    lane = lax.broadcasted_iota(jnp.int32, (side_rows, head_dim), 1)
    stats = [jnp.zeros((side_rows, head_dim), F32)] * 2
    for pair in range(heads // together):
        parts = []
        for h in range(pair * together, (pair + 1) * together):
            cols = slice(h * head_dim, (h + 1) * head_dim)
            for s in range(2):
                for m in range(first_m, first_m + count):
                    start = ((kv_id ^ m) * 2 + (blk_id ^ s)) * rows
                    parts.append(q_rot[pl.ds(pl.multiple_of(start, rows), rows), cols])
        queries = jnp.concatenate(parts, 0)
        scores = lax.dot_general(queries, keys, (((1,), (1,)), ((), ())), preferred_element_type=F32)
        masked = jnp.where(key_pos[...] <= length + token, scores, NEG)
        top = jnp.maximum(jnp.max(masked, 1, keepdims=True), 0.1 * NEG)
        weights = jnp.exp2((masked - top) * (scale * math.log2(math.e))).astype(BF16)
        total = jnp.sum(weights.astype(F32), 1, keepdims=True)
        out = jnp.dot(weights, values, preferred_element_type=F32)
        some = total > 0.0
        safe = jnp.where(some, total, 1.0)
        out = (out / safe).astype(BF16)
        log_sum = jnp.where(some, top * scale + jnp.log(safe), NEG)
        for i in range(together):
            h = pair * together + i
            cols = slice(h * head_dim, (h + 1) * head_dim)
            for s, out_ref in enumerate((ok_ref, os_ref)):
                at = i * head_rows + s * side_rows
                out_ref[:, cols] = out[at:at + side_rows]
                here = (lane % heads == h) & (lane < 3 * heads)
                stats[s] = jnp.where(here, log_sum[at:at + side_rows], stats[s])
    for stat, out_ref in zip(stats, (ok_ref, os_ref)):
        one = stat.astype(BF16).astype(F32)
        two = (stat - one).astype(BF16).astype(F32)
        stat = jnp.where(lane < heads, one, jnp.where(lane < 2 * heads, two, stat - one - two))
        out_ref[:, heads * head_dim:] = stat.astype(BF16)
    if first:
        for store in stores:
            store.wait()


def attend_first(scal, table, q, k_new, v_new, k_cache, v_cache, rows, first_m, count):
    tokens, head_dim = k_new.shape
    width = q.shape[1]
    slots, page = k_cache.shape[0], k_cache.shape[1]
    side = count * rows
    pair = np.arange(head_dim) % (head_dim // 2)
    freq = jnp.asarray((1e6 ** (-2.0 * pair / head_dim)).astype(np.float32)[None])
    return staged(
        functools.partial(attention_body, (first_m, count, rows, 4 if count == 1 else 1), True),
        [scal, table], [freq, q, k_new, v_new, k_cache, v_cache], 2,
        [
            jax.ShapeDtypeStruct(k_cache.shape, BF16),
            jax.ShapeDtypeStruct(v_cache.shape, BF16),
            jax.ShapeDtypeStruct((tokens, width), BF16),
            jax.ShapeDtypeStruct((1, slots * page), jnp.int32),
            jax.ShapeDtypeStruct((side, width + head_dim), BF16),
            jax.ShapeDtypeStruct((side, width + head_dim), BF16),
        ],
        [pltpu.SMEM((table.shape[1],), jnp.int32), pltpu.SemaphoreType.DMA((2,))],
        60, "attend_first", [HBM, HBM] + [VMEM] * 4)


def attend_next(scal, keys, values, q_rot, key_pos, rows, first_m, count):
    width, head_dim = q_rot.shape[1], keys.shape[2]
    side = count * rows
    return pl.pallas_call(
        functools.partial(attention_body, (first_m, count, rows, 1), False),
        in_specs=[SMEM] + [VMEM] * 4,
        out_specs=[VMEM] * 2,
        out_shape=[jax.ShapeDtypeStruct((side, width + head_dim), BF16)] * 2,
        compiler_params=pltpu.CompilerParams(vmem_limit_bytes=40 * 2**20),
        name="attend_next",
    )(scal, keys, values, q_rot, key_pos)


def project_body(head_dim, scal, o1, o2, wa, wb, wait_a, wait_b, *rest):
    outs, attn = rest[:-1], rest[-1]
    width = attn.shape[1]
    heads = width // head_dim
    depth, model = wa.shape
    blk_id = scal[2]
    rows = outs[0].shape[0]
    logs = []
    for o in (o1, o2):
        stat = o[:, width:].astype(F32)
        logs.append([sum(stat[:, h + i * heads:h + i * heads + 1] for i in range(3)) for h in range(heads)])
    for h in range(heads):
        cols = slice(h * head_dim, (h + 1) * head_dim)
        first, second = logs[0][h], logs[1][h]
        top = jnp.maximum(first, second)
        f1, f2 = jnp.exp(first - top), jnp.exp(second - top)
        mixed = f1 * o1[:, cols].astype(F32) + f2 * o2[:, cols].astype(F32)
        attn[:, cols] = (mixed / (f1 + f2)).astype(BF16)
    mine = attn[:, pl.ds(pl.multiple_of(blk_id * depth, depth), depth)]
    other = attn[:, pl.ds(pl.multiple_of((1 - blk_id) * depth, depth), depth)]
    wait_a()
    wait_b()
    step = model // 4
    for n in range(0, model, step):
        out = (
            jnp.dot(mine, wa[:, n:n + step], preferred_element_type=F32)
            + jnp.dot(other, wb[:, n:n + step], preferred_element_type=F32)
        ).astype(BF16)
        for i, out_ref in enumerate(outs):
            out_ref[:, n:n + step] = out[i * rows:(i + 1) * rows]


def project(scal, o1, o2, wa, wb, head_dim, count):
    rows = o1.shape[0]
    width = o1.shape[1] - head_dim
    return staged(
        functools.partial(project_body, head_dim), [scal], [o1, o2, wa, wb], 2,
        [jax.ShapeDtypeStruct((rows // count, wa.shape[1]), BF16)] * count,
        [pltpu.VMEM((rows, width), BF16)], 32, "project")


def norm_body(scal, x_ref, gain_ref, *rest):
    terms, resid_ref, pieces, held = rest[:3], rest[3], rest[4:-1], rest[-1]
    part = pieces[0].shape[1]
    resid = x_ref[...].astype(F32)
    for term in terms:
        resid = resid + term[...].astype(F32)
    resid_ref[...] = resid
    scale = lax.rsqrt(jnp.mean(resid * resid, axis=-1, keepdims=True) + 1e-05)
    held[...] = (resid * scale * gain_ref[...].astype(F32)).astype(BF16)
    for j, piece in enumerate(pieces):
        start = pl.multiple_of((scal[3] ^ j) * part, part)
        piece[...] = held[:, pl.ds(start, part)]


def norm_cut(scal, x, terms, gain, reqs):
    rows, model = terms[0].shape
    part = model // reqs
    return staged(
        norm_body, [scal], [x, gain, *terms], 0,
        [jax.ShapeDtypeStruct((rows, model), F32)]
        + [jax.ShapeDtypeStruct((rows, part), BF16)] * reqs,
        [pltpu.VMEM((rows, model), BF16)], 8, "norm_cut")


def partial_gate_up(feds, weights):
    flat = jnp.concatenate(feds, 0)
    flat = flat.reshape(-1, flat.shape[-1])
    both = jnp.concatenate(
        [jnp.dot(flat, w, preferred_element_type=F32).astype(BF16) for w in weights], 1)
    reqs, rows = feds[0].shape[:2]
    return both.reshape(len(feds), reqs, rows, -1).transpose(1, 0, 2, 3)


def down(hiddens, weights, groups):
    hidden = jnp.concatenate(hiddens, 0)
    depth = weights[0].shape[0]
    out = (
        jnp.dot(hidden[:, :depth], weights[0], preferred_element_type=F32)
        + jnp.dot(hidden[:, depth:], weights[1], preferred_element_type=F32)
    ).astype(BF16)
    out = out.reshape(len(hiddens), groups, -1, out.shape[1])
    return [out[:, m].reshape(-1, out.shape[-1]) for m in range(groups)]


def finish_body(chunks, scal, *refs):
    out_ref = refs[-1]
    for c in range(chunks):
        resid, own_a, own_b, own_c, back_x, back_y = refs[6 * c:6 * c + 6]
        rows, half = back_x.shape[0], back_x.shape[1] // 2
        here = slice(c * rows, (c + 1) * rows)
        whole = own_a[...].astype(F32) + own_b[...].astype(F32) + own_c[...].astype(F32)
        for block, side, value in (
            (0, 0, whole[:, :half]), (0, 1, whole[:, half:2 * half]),
            (1, 0, whole[:, 2 * half:3 * half]), (2, 1, whole[:, 3 * half:]),
            (1, 1, back_x[:, :half]), (3, 1, back_x[:, half:]),
            (2, 0, back_y[:, :half]), (3, 0, back_y[:, half:]),
        ):
            start = (scal[3] ^ block) * (2 * half) + side * half
            cols = pl.ds(pl.multiple_of(start, half), half)
            out_ref[here, cols] = (resid[:, cols] + value.astype(F32)).astype(BF16)


def finish(scal, parts):
    rows, model = parts[0][0].shape
    return staged(
        functools.partial(finish_body, len(parts)), [scal], [a for part in parts for a in part], 0,
        [jax.ShapeDtypeStruct((len(parts) * rows, model), BF16)], [], 8, "finish")[0]


def after(a, *others):
    return lax.optimization_barrier((a,) + others)[0]


def hidden_of(both):
    gate, up = jnp.split(both, 2, -1)
    return (jax.nn.silu(gate) * up).astype(BF16)


def reduce_four(x, axis, joint=False):
    came = swap(x[3], axis, 1)
    both = (x[2].astype(F32) + came.astype(F32)).astype(BF16)
    return [x[0], *bind(joint, swap(x[1], axis, 1), swap(both, axis, 2))], both


def halve_four(x, axis, joint=False):
    came = swap(jnp.stack([x[1], x[3]]), axis, 1)
    both = (x[2].astype(F32) + came[1].astype(F32)).astype(BF16)
    return [x[0], came[0], swap(both, axis, 2)], both


def total(terms):
    return terms[0].astype(F32) + terms[1].astype(F32) + terms[2].astype(F32)


def product(rows, weights):
    depth = weights[0][0].shape[0]
    near, far = rows[:, :depth], rows[:, depth:]
    return jnp.concatenate([
        (
            jnp.dot(near, pair[0], preferred_element_type=F32)
            + jnp.dot(far, pair[1], preferred_element_type=F32)
        ).astype(BF16)
        for pair in weights
    ], 1)


def on_device(x_resid, q_new, k_new, v_new, k_cache, v_cache, cache_len, page_table,
              wo, norm_gain, w_gate, w_up, w_down):
    reqs, kvs = lax.axis_size("req"), lax.axis_size("kv")
    rows, model = x_resid.shape[1:]
    head_dim = k_new.shape[2]
    scal = jnp.stack(
        [cache_len[0], lax.axis_index("kv"), lax.axis_index("blk"), lax.axis_index("req")]
    ).astype(jnp.int32)
    wo_far = swap(wo, "blk", 1)
    fast = reqs == 4 and kvs == 4
    first_m = kvs - 1 if fast else 0
    keys_out, values_out, q_rot, key_pos, o_keep, o_send = attend_first(
        scal, page_table, q_new[0], k_new[0], v_new[0], k_cache[0, 0], v_cache[0, 0],
        rows, first_m, kvs - first_m)
    projected = project(scal, o_keep, swap(o_send, "blk", 1), wo, wo_far, head_dim, kvs - first_m)
    if first_m:
        o_keep, o_send = attend_next(
            scal, keys_out, values_out, after(q_rot, projected[0]), key_pos, rows, 0, first_m)
        o_came = swap(o_send, "blk", 1)
        projected = [*project(scal, o_keep, o_came, wo, wo_far, head_dim, first_m), *projected]
    projected = [list(projected)]
    layer = four_way if fast else any_way
    layer_out = layer(x_resid[0], projected, scal, norm_gain[None], w_gate, w_up, w_down, reqs, kvs)
    return layer_out[None], keys_out[None, None], values_out[None, None]


def any_way(x_resid, projected, scal, gain, w_gate, w_up, w_down, reqs, kvs):
    rows, model = x_resid.shape
    part = model // reqs
    req_order = list(range(reqs.bit_length() - 1))
    kv_order = list(range(kvs.bit_length() - 1))
    gate_far, up_far, down_far = (swap(w, "blk", 1) for w in (w_gate, w_up, w_down))
    summed, _ = reduce_bits(jnp.stack(projected[0]), "kv", kv_order)
    resid = x_resid.astype(F32) + summed
    scale = lax.rsqrt(jnp.mean(resid * resid, axis=-1, keepdims=True) + 1e-05)
    cut = (resid * scale * gain.astype(F32)).astype(BF16).reshape(rows, reqs, part)
    pieces = [lax.dynamic_index_in_dim(cut, scal[3] ^ j, 1, False) for j in range(reqs)]
    fed = gather_bits(jnp.stack(trade(pieces, "req")), "kv")
    flat = fed.reshape(kvs * reqs * rows, part)
    hidden = []
    for gate_w, up_w in ((w_gate, w_up), (gate_far, up_far)):
        both = jnp.concatenate(
            [jnp.dot(flat, w, preferred_element_type=F32).astype(BF16) for w in (gate_w, up_w)], 1)
        both = both.reshape(kvs, reqs, rows, -1).transpose(1, 0, 2, 3)
        both, _ = reduce_bits(both, "req", req_order)
        every = jnp.stack(trade([hidden_of(both)] * reqs, "req"))
        hidden.append(every.reshape(reqs * kvs * rows, -1))
    out = (
        jnp.dot(hidden[0], w_down, preferred_element_type=F32)
        + jnp.dot(hidden[1], down_far, preferred_element_type=F32)
    ).astype(BF16)
    out = out.reshape(reqs, kvs, rows, part).transpose(1, 0, 2, 3)
    out, _ = reduce_bits(out, "kv", kv_order, BF16)
    came = jnp.stack(trade([out[j] for j in range(reqs)], "req"))
    mlp = [lax.dynamic_index_in_dim(came, scal[3] ^ j, 0, False) for j in range(reqs)]
    return (resid + jnp.concatenate(mlp, 1).astype(F32)).astype(BF16)


def four_way(x_resid, projected, scal, gain, w_gate, w_up, w_down, reqs, kvs):
    step, model = projected[0][0].shape
    part = model // reqs
    half = part // 2
    cuts = [w_down[:, :half], w_down[:, half:]]
    lent = [swap(cut, "req", mask) for cut, mask in zip(cuts, (1, 2))]
    summed, boths = [], []
    for sums in projected:
        if boths:
            sums[3] = after(sums[3], boths[-1])
        terms, both = reduce_four(sums, "kv", False)
        summed.append(terms)
        boths.append(both)

    resids, fed = [], []
    held = None
    for c, terms in enumerate(summed):
        if c == 0:
            terms[0] = after(terms[0], *lent)
        if held is not None:
            terms[0] = after(terms[0], *held)
        resid, *pieces = norm_cut(scal, x_resid[c * step:(c + 1) * step], terms, gain, reqs)
        resids.append(resid)
        got = jnp.stack(trade(pieces, "req", True))
        two, one = bind(True, swap(got, "kv", 2), swap(got, "kv", 1))
        three = swap(two, "kv", 1)
        fed.append([got, one, two, three])
        held = [one, two]
        gated = [two]

    gate_far, up_far = (swap(w, "blk", 1) for w in (w_gate, w_up))
    weights = [(w, swap(w, "blk", 1)) for w in (*cuts, *lent)]

    hiddens = []
    for got, one, two, three in fed:
        nears = [partial_gate_up([got, one, two], (w_gate, w_up))]
        fars = [partial_gate_up([got, one, two], (gate_far, up_far))]
        three = after(three, nears[0], fars[0])
        nears.append(partial_gate_up([three], (w_gate, w_up)))
        fars.append(partial_gate_up([three], (gate_far, up_far)))
        near, far = reduce_both_ways(nears, fars, "req")
        hidden = jnp.concatenate([hidden_of(near), hidden_of(far)], -1).reshape(kvs * step, -1)
        hiddens.append(hidden)

    owns, rests, parts = [], [], []
    for c, hidden in enumerate(hiddens):
        from_y, from_x = bind(True, swap(hidden, "req", 2), swap(hidden, "req", 1))
        first, second, over_x, over_y = weights
        own, both = reduce_four(product(hidden, weights).reshape(kvs, step, -1), "kv", False)
        from_y = after(from_y, both)
        rest = jnp.concatenate([product(from_y, (first, over_x)), product(from_x, (second, over_y))], 1)
        rest = list(rest.reshape(kvs, step, -1))
        rest[3] = after(rest[3], *own)
        rest, _ = reduce_four(rest, "kv", False)
        rest = total(rest).astype(BF16)
        rests.append(rest)
        back_y, back_x = bind(True, swap(rest[:, :part], "req", 2), swap(rest[:, part:], "req", 1))
        parts.append([resids[c], *own, back_x, back_y])
    return finish(scal, parts)


def solution(mesh):
    in_specs = (
        P("req", ("kv", "blk"), None),
        P("req", None, "kv"),
        P("req", None, "kv"),
        P("req", None, "kv"),
        P("req", "kv", "blk", None, None),
        P("req", "kv", "blk", None, None),
        P("req"),
        P("req", None),
        P(("kv", "blk"), None),
        P(),
        P("req", ("kv", "blk")),
        P("req", ("kv", "blk")),
        P(("kv", "blk"), "req"),
    )
    out_specs = (
        P("req", ("kv", "blk"), None),
        P("req", "kv", "blk", None, None),
        P("req", "kv", "blk", None, None),
    )
    return jax.shard_map(
        on_device, mesh=mesh, in_specs=in_specs, out_specs=out_specs, check_vma=False
    )
```

```python
import functools
import math

import jax
import jax.numpy as jnp
import numpy as np
from jax import lax
from jax.experimental import pallas as pl
from jax.experimental.pallas import tpu as pltpu
from jax.sharding import PartitionSpec as P

NEG = -1e30
F32 = jnp.float32
BF16 = jnp.bfloat16
VMEM = pl.BlockSpec(memory_space=pltpu.VMEM)
SMEM = pl.BlockSpec(memory_space=pltpu.SMEM)
HBM = pl.BlockSpec(memory_space=pltpu.HBM)


def staged(body, scalars, arrays, late, out_shape, scratch, limit, name, out_specs=None):
    count = len(arrays)

    def kernel(*refs):
        n = len(scalars)
        sources, refs_out = refs[n:n + count], refs[n + count:n + count + len(out_shape)]
        rest = refs[n + count + len(out_shape):]
        held, sems, extra = rest[:count], rest[count], rest[count + 1:]
        copies = [
            pltpu.make_async_copy(src, dst, sems.at[i])
            for i, (src, dst) in enumerate(zip(sources, held))
        ]
        for copy in copies:
            copy.start()
        for copy in copies[:count - late]:
            copy.wait()
        waits = [lambda copy=copy: copy.wait() for copy in copies[count - late:]]
        body(*refs[:n], *held, *waits, *refs_out, *extra)

    return pl.pallas_call(
        kernel,
        in_specs=[SMEM] * len(scalars) + [HBM] * count,
        out_specs=out_specs or [VMEM] * len(out_shape),
        out_shape=out_shape,
        scratch_shapes=[pltpu.VMEM(a.shape, a.dtype) for a in arrays]
        + [pltpu.SemaphoreType.DMA((count,))] + list(scratch),
        compiler_params=pltpu.CompilerParams(vmem_limit_bytes=limit * 2**20),
        name=name,
    )(*scalars, *arrays)


def direct(body, scalars, arrays, out_shape, scratch, limit, name):
    return pl.pallas_call(
        body,
        in_specs=[SMEM] * len(scalars) + [VMEM] * len(arrays),
        out_specs=[VMEM] * len(out_shape),
        out_shape=out_shape,
        scratch_shapes=list(scratch),
        compiler_params=pltpu.CompilerParams(vmem_limit_bytes=limit * 2**20),
        name=name,
    )(*scalars, *arrays)


def swap(a, axis, mask):
    return lax.ppermute(a, axis, [(i, i ^ mask) for i in range(lax.axis_size(axis))])


def reduce_bits(x, axis, order, last=F32):
    first = None
    count = x.shape[0]
    left = list(range(count.bit_length() - 1))[::-1]
    x = x.reshape((2,) * len(left) + x.shape[1:])
    for bit in order:
        dim = left.index(bit)
        left.remove(bit)
        kept = lax.index_in_dim(x, 0, dim, False).astype(F32)
        came = swap(lax.index_in_dim(x, 1, dim, False), axis, 1 << bit)
        x = (kept + came.astype(F32)).astype(BF16 if left else last)
        first = x if first is None else first
    return x, first


def gather_bits(x, axis):
    x = x[None]
    for bit in range(lax.axis_size(axis).bit_length() - 1)[::-1]:
        came = swap(x, axis, 1 << bit)
        x = jnp.stack([x, came], 1).reshape((2 * x.shape[0],) + x.shape[1:])
    return x


def bind(joint, *values):
    return lax.optimization_barrier(values) if joint else values


def trade(pieces, axis, joint=False):
    return [pieces[0], *bind(joint, *(swap(piece, axis, j) for j, piece in enumerate(pieces) if j))]


def reduce_both_ways(nears, fars, axis):
    sums_near, sums_far = [], []
    for near, far in zip(nears, fars):
        came = bind(len(sums_near) > 0, swap(near[1::2], axis, 1), swap(far[2:], axis, 2), *sums_near, *sums_far)
        sums_near.append((near[::2].astype(F32) + came[0].astype(F32)).astype(BF16))
        sums_far.append((far[:2].astype(F32) + came[1].astype(F32)).astype(BF16))
    near, far = jnp.concatenate(sums_near, 1), jnp.concatenate(sums_far, 1)
    more = bind(True, swap(near[1], axis, 2), swap(far[1], axis, 1))
    return near[0].astype(F32) + more[0].astype(F32), far[0].astype(F32) + more[1].astype(F32)


def attention_body(shape, first, *refs):
    first_m, count, rows, together = shape
    if first:
        (scal, table, freq, q_ref, kn_ref, vn_ref, ko_ref, vo_ref, wait_k, wait_v,
         k_out, v_out, q_rot, key_pos, ok_ref, os_ref, inverse, out_sems) = refs
        tokens, head_dim = kn_ref.shape
        pages = table.shape[1]
    else:
        scal, ko_ref, vo_ref, q_rot, key_pos, ok_ref, os_ref = refs
        tokens, head_dim = q_rot.shape[0], ko_ref.shape[2]
    slots, page = ko_ref.shape[0], ko_ref.shape[1]
    heads = q_rot.shape[1] // head_dim
    length, kv_id, blk_id = scal[0], scal[1], scal[2]
    scale = 1.0 / math.sqrt(head_dim)

    if first:
        @pl.loop(0, pages)
        def _(j):
            inverse[table[0, j]] = j

        lane = lax.broadcasted_iota(jnp.int32, (1, page), 1)
        for s in range(slots):
            key_pos[:, s * page:(s + 1) * page] = inverse[blk_id * slots + s] * page + lane

        where_at = (length + lax.broadcasted_iota(jnp.int32, (tokens, head_dim), 0)).astype(F32)
        angle = where_at * freq[...]
        cosine = jnp.cos(angle)
        sine = jnp.sin(angle)
        low = lax.broadcasted_iota(jnp.int32, (tokens, head_dim), 1) < head_dim // 2
        sine = jnp.where(low, -sine, sine)

        def rotate(u):
            u = u.astype(F32)
            return (u * cosine + pltpu.roll(u, head_dim // 2, 1) * sine).astype(BF16)

        for h in range(heads):
            cols = slice(h * head_dim, (h + 1) * head_dim)
            q_rot[:, cols] = rotate(q_ref[:, cols])
        k_rot = rotate(kn_ref[...])

        wait_k()
        wait_v()
        for extra in range(tokens // page + 1):
            logical = length // page + extra
            slot = table[0, jnp.minimum(logical, pages - 1)] - blk_id * slots

            @pl.when((logical < pages) & (slot >= 0) & (slot < slots))
            def _():
                begin = logical * page - length
                at = begin + lax.broadcasted_iota(jnp.int32, (page, tokens), 0)
                pick = (at == lax.broadcasted_iota(jnp.int32, (page, tokens), 1)).astype(BF16)
                fresh_k = jnp.dot(pick, k_rot, preferred_element_type=F32).astype(BF16)
                fresh_v = jnp.dot(pick, vn_ref[...], preferred_element_type=F32).astype(BF16)
                at = begin + lax.broadcasted_iota(jnp.int32, (page, head_dim), 0)
                is_new = (at >= 0) & (at < tokens)
                ko_ref[slot] = jnp.where(is_new, fresh_k, ko_ref[slot])
                vo_ref[slot] = jnp.where(is_new, fresh_v, vo_ref[slot])

        stores = [
            pltpu.make_async_copy(src, dst, out_sems.at[i])
            for i, (src, dst) in enumerate(((ko_ref, k_out), (vo_ref, v_out)))
        ]
        for store in stores:
            store.start()

    keys = ko_ref[...].reshape(slots * page, head_dim)
    values = vo_ref[...].reshape(slots * page, head_dim)
    side_rows = count * rows
    head_rows = 2 * side_rows
    row = lax.broadcasted_iota(jnp.int32, (together * head_rows, 1), 0) % head_rows
    side = row // side_rows
    place = (row % side_rows) // rows + first_m
    token = ((place ^ kv_id) * 2 + (blk_id ^ side)) * rows + row % rows
    lane = lax.broadcasted_iota(jnp.int32, (side_rows, head_dim), 1)
    stats = [jnp.zeros((side_rows, head_dim), F32)] * 2
    for pair in range(heads // together):
        parts = []
        for h in range(pair * together, (pair + 1) * together):
            cols = slice(h * head_dim, (h + 1) * head_dim)
            for s in range(2):
                for m in range(first_m, first_m + count):
                    start = ((kv_id ^ m) * 2 + (blk_id ^ s)) * rows
                    parts.append(q_rot[pl.ds(pl.multiple_of(start, rows), rows), cols])
        queries = jnp.concatenate(parts, 0)
        scores = lax.dot_general(queries, keys, (((1,), (1,)), ((), ())), preferred_element_type=F32)
        masked = jnp.where(key_pos[...] <= length + token, scores, NEG)
        top = jnp.maximum(jnp.max(masked, 1, keepdims=True), 0.1 * NEG)
        weights = jnp.exp2((masked - top) * (scale * math.log2(math.e))).astype(BF16)
        total = jnp.sum(weights.astype(F32), 1, keepdims=True)
        out = jnp.dot(weights, values, preferred_element_type=F32)
        some = total > 0.0
        safe = jnp.where(some, total, 1.0)
        out = (out / safe).astype(BF16)
        log_sum = jnp.where(some, top * scale + jnp.log(safe), NEG)
        for i in range(together):
            h = pair * together + i
            cols = slice(h * head_dim, (h + 1) * head_dim)
            for s, out_ref in enumerate((ok_ref, os_ref)):
                at = i * head_rows + s * side_rows
                out_ref[:, cols] = out[at:at + side_rows]
                here = (lane % heads == h) & (lane < 3 * heads)
                stats[s] = jnp.where(here, log_sum[at:at + side_rows], stats[s])
    for stat, out_ref in zip(stats, (ok_ref, os_ref)):
        one = stat.astype(BF16).astype(F32)
        two = (stat - one).astype(BF16).astype(F32)
        stat = jnp.where(lane < heads, one, jnp.where(lane < 2 * heads, two, stat - one - two))
        out_ref[:, heads * head_dim:] = stat.astype(BF16)
    if first:
        for store in stores:
            store.wait()


def attend_first(scal, table, q, k_new, v_new, k_cache, v_cache, rows, first_m, count):
    tokens, head_dim = k_new.shape
    width = q.shape[1]
    slots, page = k_cache.shape[0], k_cache.shape[1]
    side = count * rows
    pair = np.arange(head_dim) % (head_dim // 2)
    freq = jnp.asarray((1e6 ** (-2.0 * pair / head_dim)).astype(np.float32)[None])
    return staged(
        functools.partial(attention_body, (first_m, count, rows, 4 if count == 1 else 1), True),
        [scal, table], [freq, q, k_new, v_new, k_cache, v_cache], 2,
        [
            jax.ShapeDtypeStruct(k_cache.shape, BF16),
            jax.ShapeDtypeStruct(v_cache.shape, BF16),
            jax.ShapeDtypeStruct((tokens, width), BF16),
            jax.ShapeDtypeStruct((1, slots * page), jnp.int32),
            jax.ShapeDtypeStruct((side, width + head_dim), BF16),
            jax.ShapeDtypeStruct((side, width + head_dim), BF16),
        ],
        [pltpu.SMEM((table.shape[1],), jnp.int32), pltpu.SemaphoreType.DMA((2,))],
        60, "attend_first", [HBM, HBM] + [VMEM] * 4)


def attend_next(scal, keys, values, q_rot, key_pos, rows, first_m, count):
    width, head_dim = q_rot.shape[1], keys.shape[2]
    side = count * rows
    return pl.pallas_call(
        functools.partial(attention_body, (first_m, count, rows, 1), False),
        in_specs=[SMEM] + [VMEM] * 4,
        out_specs=[VMEM] * 2,
        out_shape=[jax.ShapeDtypeStruct((side, width + head_dim), BF16)] * 2,
        compiler_params=pltpu.CompilerParams(vmem_limit_bytes=40 * 2**20),
        cost_estimate=pl.CostEstimate(flops=8 * 10**9, bytes_accessed=10**6, transcendentals=0),
        name="attend_next",
    )(scal, keys, values, q_rot, key_pos)


def project_body(head_dim, scal, o1, o2, wa, wb, wait_a, wait_b, *rest):
    outs, attn = rest[:-1], rest[-1]
    width = attn.shape[1]
    heads = width // head_dim
    depth, model = wa.shape
    blk_id = scal[2]
    rows = outs[0].shape[0]
    logs = []
    for o in (o1, o2):
        stat = o[:, width:].astype(F32)
        logs.append([sum(stat[:, h + i * heads:h + i * heads + 1] for i in range(3)) for h in range(heads)])
    for h in range(heads):
        cols = slice(h * head_dim, (h + 1) * head_dim)
        first, second = logs[0][h], logs[1][h]
        top = jnp.maximum(first, second)
        f1, f2 = jnp.exp(first - top), jnp.exp(second - top)
        mixed = f1 * o1[:, cols].astype(F32) + f2 * o2[:, cols].astype(F32)
        attn[:, cols] = (mixed / (f1 + f2)).astype(BF16)
    mine = attn[:, pl.ds(pl.multiple_of(blk_id * depth, depth), depth)]
    other = attn[:, pl.ds(pl.multiple_of((1 - blk_id) * depth, depth), depth)]
    wait_a()
    wait_b()
    step = model // 4
    for n in range(0, model, step):
        out = (
            jnp.dot(mine, wa[:, n:n + step], preferred_element_type=F32)
            + jnp.dot(other, wb[:, n:n + step], preferred_element_type=F32)
        ).astype(BF16)
        for i, out_ref in enumerate(outs):
            out_ref[:, n:n + step] = out[i * rows:(i + 1) * rows]


def project(scal, o1, o2, wa, wb, head_dim, count):
    rows = o1.shape[0]
    width = o1.shape[1] - head_dim
    return staged(
        functools.partial(project_body, head_dim), [scal], [o1, o2, wa, wb], 2,
        [jax.ShapeDtypeStruct((rows // count, wa.shape[1]), BF16)] * count,
        [pltpu.VMEM((rows, width), BF16)], 32, "project")


def norm_body(scal, x_ref, gain_ref, *rest):
    terms, resid_ref, pieces, held = rest[:3], rest[3], rest[4:-1], rest[-1]
    part = pieces[0].shape[1]
    resid = x_ref[...].astype(F32)
    for term in terms:
        resid = resid + term[...].astype(F32)
    resid_ref[...] = resid
    scale = lax.rsqrt(jnp.mean(resid * resid, axis=-1, keepdims=True) + 1e-05)
    held[...] = (resid * scale * gain_ref[...].astype(F32)).astype(BF16)
    for j, piece in enumerate(pieces):
        start = pl.multiple_of((scal[3] ^ j) * part, part)
        piece[...] = held[:, pl.ds(start, part)]


def norm_cut(scal, x, terms, gain, reqs):
    rows, model = terms[0].shape
    part = model // reqs
    return staged(
        norm_body, [scal], [x, gain, *terms], 0,
        [jax.ShapeDtypeStruct((rows, model), F32)]
        + [jax.ShapeDtypeStruct((rows, part), BF16)] * reqs,
        [pltpu.VMEM((rows, model), BF16)], 8, "norm_cut")


def partial_gate_up(feds, weights):
    flat = jnp.concatenate(feds, 0)
    flat = flat.reshape(-1, flat.shape[-1])
    both = jnp.concatenate(
        [jnp.dot(flat, w, preferred_element_type=F32).astype(BF16) for w in weights], 1)
    reqs, rows = feds[0].shape[:2]
    return both.reshape(len(feds), reqs, rows, -1).transpose(1, 0, 2, 3)


def down(hiddens, weights, groups):
    hidden = jnp.concatenate(hiddens, 0)
    depth = weights[0].shape[0]
    out = (
        jnp.dot(hidden[:, :depth], weights[0], preferred_element_type=F32)
        + jnp.dot(hidden[:, depth:], weights[1], preferred_element_type=F32)
    ).astype(BF16)
    out = out.reshape(len(hiddens), groups, -1, out.shape[1])
    return [out[:, m].reshape(-1, out.shape[-1]) for m in range(groups)]


def finish_body(chunks, scal, *refs):
    out_ref = refs[-1]
    for c in range(chunks):
        resid, own_a, own_b, own_c, back_x, back_y = refs[6 * c:6 * c + 6]
        rows, half = back_x.shape[0], back_x.shape[1] // 2
        here = slice(c * rows, (c + 1) * rows)
        whole = own_a[...].astype(F32) + own_b[...].astype(F32) + own_c[...].astype(F32)
        for block, side, value in (
            (0, 0, whole[:, :half]), (0, 1, whole[:, half:2 * half]),
            (1, 0, whole[:, 2 * half:3 * half]), (2, 1, whole[:, 3 * half:]),
            (1, 1, back_x[:, :half]), (3, 1, back_x[:, half:]),
            (2, 0, back_y[:, :half]), (3, 0, back_y[:, half:]),
        ):
            start = (scal[3] ^ block) * (2 * half) + side * half
            cols = pl.ds(pl.multiple_of(start, half), half)
            out_ref[here, cols] = (resid[:, cols] + value.astype(F32)).astype(BF16)


def finish(scal, parts):
    rows, model = parts[0][0].shape
    return direct(
        functools.partial(finish_body, len(parts)), [scal], [a for part in parts for a in part],
        [jax.ShapeDtypeStruct((len(parts) * rows, model), BF16)], [], 8, "finish")[0]


def after(a, *others):
    return lax.optimization_barrier((a,) + others)[0]


def hidden_of(both):
    gate, up = jnp.split(both, 2, -1)
    return (jax.nn.silu(gate) * up).astype(BF16)


def reduce_four(x, axis, joint=False):
    came = swap(x[3], axis, 1)
    both = (x[2].astype(F32) + came.astype(F32)).astype(BF16)
    return [x[0], *bind(joint, swap(x[1], axis, 1), swap(both, axis, 2))], both


def halve_four(x, axis, joint=False):
    came = swap(jnp.stack([x[1], x[3]]), axis, 1)
    both = (x[2].astype(F32) + came[1].astype(F32)).astype(BF16)
    return [x[0], came[0], swap(both, axis, 2)], both


def total(terms):
    return terms[0].astype(F32) + terms[1].astype(F32) + terms[2].astype(F32)


def product(rows, weights):
    depth = weights[0][0].shape[0]
    near, far = rows[:, :depth], rows[:, depth:]
    return jnp.concatenate([
        (
            jnp.dot(near, pair[0], preferred_element_type=F32)
            + jnp.dot(far, pair[1], preferred_element_type=F32)
        ).astype(BF16)
        for pair in weights
    ], 1)


def on_device(x_resid, q_new, k_new, v_new, k_cache, v_cache, cache_len, page_table,
              wo, norm_gain, w_gate, w_up, w_down):
    reqs, kvs = lax.axis_size("req"), lax.axis_size("kv")
    rows, model = x_resid.shape[1:]
    head_dim = k_new.shape[2]
    scal = jnp.stack(
        [cache_len[0], lax.axis_index("kv"), lax.axis_index("blk"), lax.axis_index("req")]
    ).astype(jnp.int32)
    wo_far = swap(wo, "blk", 1)
    fast = reqs == 4 and kvs == 4
    half = model // reqs // 2
    cuts = [w_down[:, :half], w_down[:, half:]]
    first_m = kvs - 1 if fast else 0
    keys_out, values_out, q_rot, key_pos, o_keep, o_send = attend_first(
        scal, page_table, q_new[0], k_new[0], v_new[0], k_cache[0, 0], v_cache[0, 0],
        rows, first_m, kvs - first_m)
    projected = project(scal, o_keep, swap(o_send, "blk", 1), wo, wo_far, head_dim, kvs - first_m)
    if first_m:
        o_keep, o_send = attend_next(
            scal, keys_out, values_out, after(q_rot, projected[0], *cuts), key_pos, rows, 0, first_m)
        o_came = swap(o_send, "blk", 1)
        projected = [*project(scal, o_keep, o_came, wo, wo_far, head_dim, first_m), *projected]
    projected = [list(projected)]
    layer = four_way if fast else any_way
    layer_out = layer(x_resid[0], projected, scal, norm_gain[None], w_gate, w_up, cuts if fast else w_down, reqs, kvs)
    return layer_out[None], keys_out[None, None], values_out[None, None]


def any_way(x_resid, projected, scal, gain, w_gate, w_up, w_down, reqs, kvs):
    rows, model = x_resid.shape
    part = model // reqs
    req_order = list(range(reqs.bit_length() - 1))
    kv_order = list(range(kvs.bit_length() - 1))
    gate_far, up_far, down_far = (swap(w, "blk", 1) for w in (w_gate, w_up, w_down))
    summed, _ = reduce_bits(jnp.stack(projected[0]), "kv", kv_order)
    resid = x_resid.astype(F32) + summed
    scale = lax.rsqrt(jnp.mean(resid * resid, axis=-1, keepdims=True) + 1e-05)
    cut = (resid * scale * gain.astype(F32)).astype(BF16).reshape(rows, reqs, part)
    pieces = [lax.dynamic_index_in_dim(cut, scal[3] ^ j, 1, False) for j in range(reqs)]
    fed = gather_bits(jnp.stack(trade(pieces, "req")), "kv")
    flat = fed.reshape(kvs * reqs * rows, part)
    hidden = []
    for gate_w, up_w in ((w_gate, w_up), (gate_far, up_far)):
        both = jnp.concatenate(
            [jnp.dot(flat, w, preferred_element_type=F32).astype(BF16) for w in (gate_w, up_w)], 1)
        both = both.reshape(kvs, reqs, rows, -1).transpose(1, 0, 2, 3)
        both, _ = reduce_bits(both, "req", req_order)
        every = jnp.stack(trade([hidden_of(both)] * reqs, "req"))
        hidden.append(every.reshape(reqs * kvs * rows, -1))
    out = (
        jnp.dot(hidden[0], w_down, preferred_element_type=F32)
        + jnp.dot(hidden[1], down_far, preferred_element_type=F32)
    ).astype(BF16)
    out = out.reshape(reqs, kvs, rows, part).transpose(1, 0, 2, 3)
    out, _ = reduce_bits(out, "kv", kv_order, BF16)
    came = jnp.stack(trade([out[j] for j in range(reqs)], "req"))
    mlp = [lax.dynamic_index_in_dim(came, scal[3] ^ j, 0, False) for j in range(reqs)]
    return (resid + jnp.concatenate(mlp, 1).astype(F32)).astype(BF16)


def four_way(x_resid, projected, scal, gain, w_gate, w_up, cuts, reqs, kvs):
    step, model = projected[0][0].shape
    part = model // reqs
    half = part // 2
    lent = [swap(cut, "req", mask) for cut, mask in zip(cuts, (1, 2))]
    summed, boths = [], []
    for sums in projected:
        if boths:
            sums[3] = after(sums[3], boths[-1])
        terms, both = reduce_four(sums, "kv", False)
        summed.append(terms)
        boths.append(both)

    resids, fed = [], []
    held = None
    for c, terms in enumerate(summed):
        if held is not None:
            terms[0] = after(terms[0], *held)
        resid, *pieces = norm_cut(scal, x_resid[c * step:(c + 1) * step], terms, gain, reqs)
        resids.append(resid)
        pieces[1:] = [after(piece, *lent) for piece in pieces[1:]]
        got = jnp.stack(trade(pieces, "req", True))
        two, one = bind(True, swap(got, "kv", 2), swap(got, "kv", 1))
        three = swap(two, "kv", 1)
        fed.append([got, one, two, three])
        held = [one, two]
        gated = [two]

    gate_far, up_far = (swap(w, "blk", 1) for w in (w_gate, w_up))
    weights = [(w, swap(w, "blk", 1)) for w in (*cuts, *lent)]

    hiddens = []
    for got, one, two, three in fed:
        nears = [partial_gate_up([got, one, two], (w_gate, w_up))]
        fars = [partial_gate_up([got, one, two], (gate_far, up_far))]
        three = after(three, nears[0], fars[0])
        nears.append(partial_gate_up([three], (w_gate, w_up)))
        fars.append(partial_gate_up([three], (gate_far, up_far)))
        near, far = reduce_both_ways(nears, fars, "req")
        hidden = jnp.concatenate([hidden_of(near), hidden_of(far)], -1).reshape(kvs * step, -1)
        hiddens.append(hidden)

    owns, rests, parts = [], [], []
    for c, hidden in enumerate(hiddens):
        from_y, from_x = bind(True, swap(hidden, "req", 2), swap(hidden, "req", 1))
        first, second, over_x, over_y = weights
        own, both = reduce_four(product(hidden, weights).reshape(kvs, step, -1), "kv", False)
        from_y = after(from_y, both)
        rest = jnp.concatenate([product(from_y, (first, over_x)), product(from_x, (second, over_y))], 1)
        rest = list(rest.reshape(kvs, step, -1))
        rest[3] = after(rest[3], *own)
        rest, _ = reduce_four(rest, "kv", False)
        rest = total(rest).astype(BF16)
        rests.append(rest)
        back_y, back_x = bind(True, swap(rest[:, :part], "req", 2), swap(rest[:, part:], "req", 1))
        parts.append([resids[c], *own, back_x, back_y])
    return finish(scal, parts)


def solution(mesh):
    in_specs = (
        P("req", ("kv", "blk"), None),
        P("req", None, "kv"),
        P("req", None, "kv"),
        P("req", None, "kv"),
        P("req", "kv", "blk", None, None),
        P("req", "kv", "blk", None, None),
        P("req"),
        P("req", None),
        P(("kv", "blk"), None),
        P(),
        P("req", ("kv", "blk")),
        P("req", ("kv", "blk")),
        P(("kv", "blk"), "req"),
    )
    out_specs = (
        P("req", ("kv", "blk"), None),
        P("req", "kv", "blk", None, None),
        P("req", "kv", "blk", None, None),
    )
    return jax.shard_map(
        on_device, mesh=mesh, in_specs=in_specs, out_specs=out_specs, check_vma=False
    )
```

```python
import functools
import math

import jax
import jax.numpy as jnp
import numpy as np
from jax import lax
from jax.experimental import pallas as pl
from jax.experimental.pallas import tpu as pltpu
from jax.sharding import PartitionSpec as P

NEG = -1e30
F32 = jnp.float32
BF16 = jnp.bfloat16
VMEM = pl.BlockSpec(memory_space=pltpu.VMEM)
SMEM = pl.BlockSpec(memory_space=pltpu.SMEM)
HBM = pl.BlockSpec(memory_space=pltpu.HBM)


def staged(body, scalars, arrays, late, out_shape, scratch, limit, name, out_specs=None):
    count = len(arrays)

    def kernel(*refs):
        n = len(scalars)
        sources, refs_out = refs[n:n + count], refs[n + count:n + count + len(out_shape)]
        rest = refs[n + count + len(out_shape):]
        held, sems, extra = rest[:count], rest[count], rest[count + 1:]
        copies = [
            pltpu.make_async_copy(src, dst, sems.at[i])
            for i, (src, dst) in enumerate(zip(sources, held))
        ]
        for copy in copies:
            copy.start()
        for copy in copies[:count - late]:
            copy.wait()
        waits = [lambda copy=copy: copy.wait() for copy in copies[count - late:]]
        body(*refs[:n], *held, *waits, *refs_out, *extra)

    return pl.pallas_call(
        kernel,
        in_specs=[SMEM] * len(scalars) + [HBM] * count,
        out_specs=out_specs or [VMEM] * len(out_shape),
        out_shape=out_shape,
        scratch_shapes=[pltpu.VMEM(a.shape, a.dtype) for a in arrays]
        + [pltpu.SemaphoreType.DMA((count,))] + list(scratch),
        compiler_params=pltpu.CompilerParams(vmem_limit_bytes=limit * 2**20),
        name=name,
    )(*scalars, *arrays)


def direct(body, scalars, arrays, out_shape, scratch, limit, name):
    return pl.pallas_call(
        body,
        in_specs=[SMEM] * len(scalars) + [VMEM] * len(arrays),
        out_specs=[VMEM] * len(out_shape),
        out_shape=out_shape,
        scratch_shapes=list(scratch),
        compiler_params=pltpu.CompilerParams(vmem_limit_bytes=limit * 2**20),
        name=name,
    )(*scalars, *arrays)


def swap(a, axis, mask):
    return lax.ppermute(a, axis, [(i, i ^ mask) for i in range(lax.axis_size(axis))])


def reduce_bits(x, axis, order, last=F32):
    first = None
    count = x.shape[0]
    left = list(range(count.bit_length() - 1))[::-1]
    x = x.reshape((2,) * len(left) + x.shape[1:])
    for bit in order:
        dim = left.index(bit)
        left.remove(bit)
        kept = lax.index_in_dim(x, 0, dim, False).astype(F32)
        came = swap(lax.index_in_dim(x, 1, dim, False), axis, 1 << bit)
        x = (kept + came.astype(F32)).astype(BF16 if left else last)
        first = x if first is None else first
    return x, first


def gather_bits(x, axis):
    x = x[None]
    for bit in range(lax.axis_size(axis).bit_length() - 1)[::-1]:
        came = swap(x, axis, 1 << bit)
        x = jnp.stack([x, came], 1).reshape((2 * x.shape[0],) + x.shape[1:])
    return x


def bind(joint, *values):
    return lax.optimization_barrier(values) if joint else values


def trade(pieces, axis, joint=False):
    return [pieces[0], *bind(joint, *(swap(piece, axis, j) for j, piece in enumerate(pieces) if j))]


def reduce_both_ways(nears, fars, axis):
    sums_near, sums_far = [], []
    for near, far in zip(nears, fars):
        came = bind(len(sums_near) > 0, swap(near[1::2], axis, 1), swap(far[2:], axis, 2), *sums_near, *sums_far)
        sums_near.append((near[::2].astype(F32) + came[0].astype(F32)).astype(BF16))
        sums_far.append((far[:2].astype(F32) + came[1].astype(F32)).astype(BF16))
    near, far = jnp.concatenate(sums_near, 1), jnp.concatenate(sums_far, 1)
    more = bind(True, swap(near[1], axis, 2), swap(far[1], axis, 1))
    return near[0].astype(F32) + more[0].astype(F32), far[0].astype(F32) + more[1].astype(F32)


def attention_body(shape, first, *refs):
    first_m, count, rows, together = shape
    if first:
        (scal, table, freq, q_ref, kn_ref, vn_ref, ko_ref, vo_ref, wait_k, wait_v,
         k_out, v_out, q_rot, key_pos, ok_ref, os_ref, inverse, out_sems) = refs
        tokens, head_dim = kn_ref.shape
        pages = table.shape[1]
    else:
        scal, ko_ref, vo_ref, q_rot, key_pos, ok_ref, os_ref = refs
        tokens, head_dim = q_rot.shape[0], ko_ref.shape[2]
    slots, page = ko_ref.shape[0], ko_ref.shape[1]
    heads = q_rot.shape[1] // head_dim
    length, kv_id, blk_id = scal[0], scal[1], scal[2]
    scale = 1.0 / math.sqrt(head_dim)

    if first:
        @pl.loop(0, pages)
        def _(j):
            inverse[table[0, j]] = j

        lane = lax.broadcasted_iota(jnp.int32, (1, page), 1)
        for s in range(slots):
            key_pos[:, s * page:(s + 1) * page] = inverse[blk_id * slots + s] * page + lane

        where_at = (length + lax.broadcasted_iota(jnp.int32, (tokens, head_dim), 0)).astype(F32)
        angle = where_at * freq[...]
        cosine = jnp.cos(angle)
        sine = jnp.sin(angle)
        low = lax.broadcasted_iota(jnp.int32, (tokens, head_dim), 1) < head_dim // 2
        sine = jnp.where(low, -sine, sine)

        def rotate(u):
            u = u.astype(F32)
            return (u * cosine + pltpu.roll(u, head_dim // 2, 1) * sine).astype(BF16)

        for h in range(heads):
            cols = slice(h * head_dim, (h + 1) * head_dim)
            q_rot[:, cols] = rotate(q_ref[:, cols])
        k_rot = rotate(kn_ref[...])

        wait_k()
        wait_v()
        for extra in range(tokens // page + 1):
            logical = length // page + extra
            slot = table[0, jnp.minimum(logical, pages - 1)] - blk_id * slots

            @pl.when((logical < pages) & (slot >= 0) & (slot < slots))
            def _():
                begin = logical * page - length
                at = begin + lax.broadcasted_iota(jnp.int32, (page, tokens), 0)
                pick = (at == lax.broadcasted_iota(jnp.int32, (page, tokens), 1)).astype(BF16)
                fresh_k = jnp.dot(pick, k_rot, preferred_element_type=F32).astype(BF16)
                fresh_v = jnp.dot(pick, vn_ref[...], preferred_element_type=F32).astype(BF16)
                at = begin + lax.broadcasted_iota(jnp.int32, (page, head_dim), 0)
                is_new = (at >= 0) & (at < tokens)
                ko_ref[slot] = jnp.where(is_new, fresh_k, ko_ref[slot])
                vo_ref[slot] = jnp.where(is_new, fresh_v, vo_ref[slot])

        stores = [
            pltpu.make_async_copy(src, dst, out_sems.at[i])
            for i, (src, dst) in enumerate(((ko_ref, k_out), (vo_ref, v_out)))
        ]
        for store in stores:
            store.start()

    keys = ko_ref[...].reshape(slots * page, head_dim)
    values = vo_ref[...].reshape(slots * page, head_dim)
    side_rows = count * rows
    head_rows = 2 * side_rows
    row = lax.broadcasted_iota(jnp.int32, (together * head_rows, 1), 0) % head_rows
    side = row // side_rows
    place = (row % side_rows) // rows + first_m
    token = ((place ^ kv_id) * 2 + (blk_id ^ side)) * rows + row % rows
    lane = lax.broadcasted_iota(jnp.int32, (side_rows, head_dim), 1)
    stats = [jnp.zeros((side_rows, head_dim), F32)] * 2
    for pair in range(heads // together):
        parts = []
        for h in range(pair * together, (pair + 1) * together):
            cols = slice(h * head_dim, (h + 1) * head_dim)
            for s in range(2):
                for m in range(first_m, first_m + count):
                    start = ((kv_id ^ m) * 2 + (blk_id ^ s)) * rows
                    parts.append(q_rot[pl.ds(pl.multiple_of(start, rows), rows), cols])
        queries = jnp.concatenate(parts, 0)
        scores = lax.dot_general(queries, keys, (((1,), (1,)), ((), ())), preferred_element_type=F32)
        masked = jnp.where(key_pos[...] <= length + token, scores, NEG)
        top = jnp.maximum(jnp.max(masked, 1, keepdims=True), 0.1 * NEG)
        weights = jnp.exp2((masked - top) * (scale * math.log2(math.e))).astype(BF16)
        total = jnp.sum(weights.astype(F32), 1, keepdims=True)
        out = jnp.dot(weights, values, preferred_element_type=F32)
        some = total > 0.0
        safe = jnp.where(some, total, 1.0)
        out = (out / safe).astype(BF16)
        log_sum = jnp.where(some, top * scale + jnp.log(safe), NEG)
        for i in range(together):
            h = pair * together + i
            cols = slice(h * head_dim, (h + 1) * head_dim)
            for s, out_ref in enumerate((ok_ref, os_ref)):
                at = i * head_rows + s * side_rows
                out_ref[:, cols] = out[at:at + side_rows]
                here = (lane % heads == h) & (lane < 3 * heads)
                stats[s] = jnp.where(here, log_sum[at:at + side_rows], stats[s])
    for stat, out_ref in zip(stats, (ok_ref, os_ref)):
        one = stat.astype(BF16).astype(F32)
        two = (stat - one).astype(BF16).astype(F32)
        stat = jnp.where(lane < heads, one, jnp.where(lane < 2 * heads, two, stat - one - two))
        out_ref[:, heads * head_dim:] = stat.astype(BF16)
    if first:
        for store in stores:
            store.wait()


def attend_first(scal, table, q, k_new, v_new, k_cache, v_cache, rows, first_m, count):
    tokens, head_dim = k_new.shape
    width = q.shape[1]
    slots, page = k_cache.shape[0], k_cache.shape[1]
    side = count * rows
    pair = np.arange(head_dim) % (head_dim // 2)
    freq = jnp.asarray((1e6 ** (-2.0 * pair / head_dim)).astype(np.float32)[None])
    return staged(
        functools.partial(attention_body, (first_m, count, rows, 4 if count == 1 else 1), True),
        [scal, table], [freq, q, k_new, v_new, k_cache, v_cache], 2,
        [
            jax.ShapeDtypeStruct(k_cache.shape, BF16),
            jax.ShapeDtypeStruct(v_cache.shape, BF16),
            jax.ShapeDtypeStruct((tokens, width), BF16),
            jax.ShapeDtypeStruct((1, slots * page), jnp.int32),
            jax.ShapeDtypeStruct((side, width + head_dim), BF16),
            jax.ShapeDtypeStruct((side, width + head_dim), BF16),
        ],
        [pltpu.SMEM((table.shape[1],), jnp.int32), pltpu.SemaphoreType.DMA((2,))],
        56, "attend_first", [HBM, HBM] + [VMEM] * 4)


def attend_next(scal, keys, values, q_rot, key_pos, rows, first_m, count):
    width, head_dim = q_rot.shape[1], keys.shape[2]
    side = count * rows
    return pl.pallas_call(
        functools.partial(attention_body, (first_m, count, rows, 1), False),
        in_specs=[SMEM] + [VMEM] * 4,
        out_specs=[VMEM] * 2,
        out_shape=[jax.ShapeDtypeStruct((side, width + head_dim), BF16)] * 2,
        compiler_params=pltpu.CompilerParams(vmem_limit_bytes=40 * 2**20),
        cost_estimate=pl.CostEstimate(flops=8 * 10**9, bytes_accessed=10**6, transcendentals=0),
        name="attend_next",
    )(scal, keys, values, q_rot, key_pos)


def project_body(head_dim, scal, o1, o2, wa, wb, *rest):
    outs, attn = rest[:-1], rest[-1]
    width = attn.shape[1]
    heads = width // head_dim
    depth, model = wa.shape
    blk_id = scal[2]
    rows = outs[0].shape[0]
    logs = []
    for o in (o1, o2):
        stat = o[:, width:].astype(F32)
        logs.append([sum(stat[:, h + i * heads:h + i * heads + 1] for i in range(3)) for h in range(heads)])
    for h in range(heads):
        cols = slice(h * head_dim, (h + 1) * head_dim)
        first, second = logs[0][h], logs[1][h]
        top = jnp.maximum(first, second)
        f1, f2 = jnp.exp(first - top), jnp.exp(second - top)
        mixed = f1 * o1[:, cols].astype(F32) + f2 * o2[:, cols].astype(F32)
        attn[:, cols] = (mixed / (f1 + f2)).astype(BF16)
    mine = attn[:, pl.ds(pl.multiple_of(blk_id * depth, depth), depth)]
    other = attn[:, pl.ds(pl.multiple_of((1 - blk_id) * depth, depth), depth)]
    step = model // 4
    for n in range(0, model, step):
        out = (
            jnp.dot(mine, wa[:, n:n + step], preferred_element_type=F32)
            + jnp.dot(other, wb[:, n:n + step], preferred_element_type=F32)
        ).astype(BF16)
        for i, out_ref in enumerate(outs):
            out_ref[:, n:n + step] = out[i * rows:(i + 1) * rows]


def project(scal, o1, o2, wa, wb, head_dim, count):
    rows = o1.shape[0]
    width = o1.shape[1] - head_dim
    return direct(
        functools.partial(project_body, head_dim), [scal], [o1, o2, wa, wb],
        [jax.ShapeDtypeStruct((rows // count, wa.shape[1]), BF16)] * count,
        [pltpu.VMEM((rows, width), BF16)], 32, "project")


def norm_body(scal, x_ref, gain_ref, *rest):
    terms, resid_ref, pieces, held = rest[:3], rest[3], rest[4:-1], rest[-1]
    part = pieces[0].shape[1]
    resid = x_ref[...].astype(F32)
    for term in terms:
        resid = resid + term[...].astype(F32)
    resid_ref[...] = resid
    scale = lax.rsqrt(jnp.mean(resid * resid, axis=-1, keepdims=True) + 1e-05)
    held[...] = (resid * scale * gain_ref[...].astype(F32)).astype(BF16)
    for j, piece in enumerate(pieces):
        start = pl.multiple_of((scal[3] ^ j) * part, part)
        piece[...] = held[:, pl.ds(start, part)]


def norm_cut(scal, x, terms, gain, reqs):
    rows, model = terms[0].shape
    part = model // reqs
    return direct(
        norm_body, [scal], [x, gain, *terms],
        [jax.ShapeDtypeStruct((rows, model), F32)]
        + [jax.ShapeDtypeStruct((rows, part), BF16)] * reqs,
        [pltpu.VMEM((rows, model), BF16)], 8, "norm_cut")


def partial_gate_up(feds, weights):
    flat = jnp.concatenate(feds, 0)
    flat = flat.reshape(-1, flat.shape[-1])
    both = jnp.concatenate(
        [jnp.dot(flat, w, preferred_element_type=F32).astype(BF16) for w in weights], 1)
    reqs, rows = feds[0].shape[:2]
    return both.reshape(len(feds), reqs, rows, -1).transpose(1, 0, 2, 3)


def down(hiddens, weights, groups):
    hidden = jnp.concatenate(hiddens, 0)
    depth = weights[0].shape[0]
    out = (
        jnp.dot(hidden[:, :depth], weights[0], preferred_element_type=F32)
        + jnp.dot(hidden[:, depth:], weights[1], preferred_element_type=F32)
    ).astype(BF16)
    out = out.reshape(len(hiddens), groups, -1, out.shape[1])
    return [out[:, m].reshape(-1, out.shape[-1]) for m in range(groups)]


def finish_body(chunks, scal, *refs):
    out_ref = refs[-1]
    for c in range(chunks):
        resid, own_a, own_b, own_c, back_x, back_y = refs[6 * c:6 * c + 6]
        rows, half = back_x.shape[0], back_x.shape[1] // 2
        here = slice(c * rows, (c + 1) * rows)
        whole = own_a[...].astype(F32) + own_b[...].astype(F32) + own_c[...].astype(F32)
        for block, side, value in (
            (0, 0, whole[:, :half]), (0, 1, whole[:, half:2 * half]),
            (1, 0, whole[:, 2 * half:3 * half]), (2, 1, whole[:, 3 * half:]),
            (1, 1, back_x[:, :half]), (3, 1, back_x[:, half:]),
            (2, 0, back_y[:, :half]), (3, 0, back_y[:, half:]),
        ):
            start = (scal[3] ^ block) * (2 * half) + side * half
            cols = pl.ds(pl.multiple_of(start, half), half)
            out_ref[here, cols] = (resid[:, cols] + value.astype(F32)).astype(BF16)


def finish(scal, parts):
    rows, model = parts[0][0].shape
    return direct(
        functools.partial(finish_body, len(parts)), [scal], [a for part in parts for a in part],
        [jax.ShapeDtypeStruct((len(parts) * rows, model), BF16)], [], 8, "finish")[0]


def after(a, *others):
    return lax.optimization_barrier((a,) + others)[0]


def hidden_of(both):
    gate, up = jnp.split(both, 2, -1)
    return (jax.nn.silu(gate) * up).astype(BF16)


def reduce_four(x, axis, joint=False):
    came = swap(x[3], axis, 1)
    both = (x[2].astype(F32) + came.astype(F32)).astype(BF16)
    return [x[0], *bind(joint, swap(x[1], axis, 1), swap(both, axis, 2))], both


def halve_four(x, axis, joint=False):
    came = swap(jnp.stack([x[1], x[3]]), axis, 1)
    both = (x[2].astype(F32) + came[1].astype(F32)).astype(BF16)
    return [x[0], came[0], swap(both, axis, 2)], both


def total(terms):
    return terms[0].astype(F32) + terms[1].astype(F32) + terms[2].astype(F32)


def product(rows, weights):
    depth = weights[0][0].shape[0]
    near, far = rows[:, :depth], rows[:, depth:]
    return jnp.concatenate([
        (
            jnp.dot(near, pair[0], preferred_element_type=F32)
            + jnp.dot(far, pair[1], preferred_element_type=F32)
        ).astype(BF16)
        for pair in weights
    ], 1)


def on_device(x_resid, q_new, k_new, v_new, k_cache, v_cache, cache_len, page_table,
              wo, norm_gain, w_gate, w_up, w_down):
    reqs, kvs = lax.axis_size("req"), lax.axis_size("kv")
    rows, model = x_resid.shape[1:]
    head_dim = k_new.shape[2]
    scal = jnp.stack(
        [cache_len[0], lax.axis_index("kv"), lax.axis_index("blk"), lax.axis_index("req")]
    ).astype(jnp.int32)
    wo_far = swap(wo, "blk", 1)
    fast = reqs == 4 and kvs == 4
    half = model // reqs // 2
    cuts = [w_down[:, :half], w_down[:, half:]]
    first_m = kvs - 1 if fast else 0
    keys_out, values_out, q_rot, key_pos, o_keep, o_send = attend_first(
        scal, page_table, q_new[0], k_new[0], v_new[0], k_cache[0, 0], v_cache[0, 0],
        rows, first_m, kvs - first_m)
    projected = project(scal, o_keep, swap(o_send, "blk", 1), wo, wo_far, head_dim, kvs - first_m)
    if first_m:
        o_keep, o_send = attend_next(
            scal, keys_out, values_out, after(q_rot, projected[0], *cuts), key_pos, rows, 0, first_m)
        o_came = swap(o_send, "blk", 1)
        projected = [*project(scal, o_keep, o_came, wo, wo_far, head_dim, first_m), *projected]
    projected = [list(projected)]
    layer = four_way if fast else any_way
    layer_out = layer(x_resid[0], projected, scal, norm_gain[None], w_gate, w_up, cuts if fast else w_down, reqs, kvs)
    return layer_out[None], keys_out[None, None], values_out[None, None]


def any_way(x_resid, projected, scal, gain, w_gate, w_up, w_down, reqs, kvs):
    rows, model = x_resid.shape
    part = model // reqs
    req_order = list(range(reqs.bit_length() - 1))
    kv_order = list(range(kvs.bit_length() - 1))
    gate_far, up_far, down_far = (swap(w, "blk", 1) for w in (w_gate, w_up, w_down))
    summed, _ = reduce_bits(jnp.stack(projected[0]), "kv", kv_order)
    resid = x_resid.astype(F32) + summed
    scale = lax.rsqrt(jnp.mean(resid * resid, axis=-1, keepdims=True) + 1e-05)
    cut = (resid * scale * gain.astype(F32)).astype(BF16).reshape(rows, reqs, part)
    pieces = [lax.dynamic_index_in_dim(cut, scal[3] ^ j, 1, False) for j in range(reqs)]
    fed = gather_bits(jnp.stack(trade(pieces, "req")), "kv")
    flat = fed.reshape(kvs * reqs * rows, part)
    hidden = []
    for gate_w, up_w in ((w_gate, w_up), (gate_far, up_far)):
        both = jnp.concatenate(
            [jnp.dot(flat, w, preferred_element_type=F32).astype(BF16) for w in (gate_w, up_w)], 1)
        both = both.reshape(kvs, reqs, rows, -1).transpose(1, 0, 2, 3)
        both, _ = reduce_bits(both, "req", req_order)
        every = jnp.stack(trade([hidden_of(both)] * reqs, "req"))
        hidden.append(every.reshape(reqs * kvs * rows, -1))
    out = (
        jnp.dot(hidden[0], w_down, preferred_element_type=F32)
        + jnp.dot(hidden[1], down_far, preferred_element_type=F32)
    ).astype(BF16)
    out = out.reshape(reqs, kvs, rows, part).transpose(1, 0, 2, 3)
    out, _ = reduce_bits(out, "kv", kv_order, BF16)
    came = jnp.stack(trade([out[j] for j in range(reqs)], "req"))
    mlp = [lax.dynamic_index_in_dim(came, scal[3] ^ j, 0, False) for j in range(reqs)]
    return (resid + jnp.concatenate(mlp, 1).astype(F32)).astype(BF16)


def four_way(x_resid, projected, scal, gain, w_gate, w_up, cuts, reqs, kvs):
    step, model = projected[0][0].shape
    part = model // reqs
    half = part // 2
    lent = [swap(cut, "req", mask) for cut, mask in zip(cuts, (1, 2))]
    summed, boths = [], []
    for sums in projected:
        if boths:
            sums[3] = after(sums[3], boths[-1])
        terms, both = reduce_four(sums, "kv", False)
        summed.append(terms)
        boths.append(both)

    resids, fed = [], []
    held = None
    for c, terms in enumerate(summed):
        if held is not None:
            terms[0] = after(terms[0], *held)
        resid, *pieces = norm_cut(scal, x_resid[c * step:(c + 1) * step], terms, gain, reqs)
        resids.append(resid)
        pieces[1:] = [after(piece, *lent) for piece in pieces[1:]]
        got = jnp.stack(trade(pieces, "req", True))
        two, one = bind(True, swap(got, "kv", 2), swap(got, "kv", 1))
        three = swap(two, "kv", 1)
        fed.append([got, one, two, three])
        held = [one, two]
        gated = [two]

    gate_far, up_far = (swap(w, "blk", 1) for w in (w_gate, w_up))
    weights = [(w, swap(w, "blk", 1)) for w in (*cuts, *lent)]

    hiddens = []
    for got, one, two, three in fed:
        nears = [partial_gate_up([got, one, two], (w_gate, w_up))]
        fars = [partial_gate_up([got, one, two], (gate_far, up_far))]
        three = after(three, nears[0], fars[0])
        nears.append(partial_gate_up([three], (w_gate, w_up)))
        fars.append(partial_gate_up([three], (gate_far, up_far)))
        near, far = reduce_both_ways(nears, fars, "req")
        hidden = jnp.concatenate([hidden_of(near), hidden_of(far)], -1).reshape(kvs * step, -1)
        hiddens.append(hidden)

    owns, rests, parts = [], [], []
    for c, hidden in enumerate(hiddens):
        from_y, from_x = bind(True, swap(hidden, "req", 2), swap(hidden, "req", 1))
        first, second, over_x, over_y = weights
        own, both = reduce_four(product(hidden, weights).reshape(kvs, step, -1), "kv", False)
        from_y = after(from_y, both)
        rest = jnp.concatenate([product(from_y, (first, over_x)), product(from_x, (second, over_y))], 1)
        rest = list(rest.reshape(kvs, step, -1))
        rest[3] = after(rest[3], *own)
        rest, _ = reduce_four(rest, "kv", False)
        rest = total(rest).astype(BF16)
        rests.append(rest)
        back_y, back_x = bind(True, swap(rest[:, :part], "req", 2), swap(rest[:, part:], "req", 1))
        parts.append([resids[c], *own, back_x, back_y])
    return finish(scal, parts)


def solution(mesh):
    in_specs = (
        P("req", ("kv", "blk"), None),
        P("req", None, "kv"),
        P("req", None, "kv"),
        P("req", None, "kv"),
        P("req", "kv", "blk", None, None),
        P("req", "kv", "blk", None, None),
        P("req"),
        P("req", None),
        P(("kv", "blk"), None),
        P(),
        P("req", ("kv", "blk")),
        P("req", ("kv", "blk")),
        P(("kv", "blk"), "req"),
    )
    out_specs = (
        P("req", ("kv", "blk"), None),
        P("req", "kv", "blk", None, None),
        P("req", "kv", "blk", None, None),
    )
    return jax.shard_map(
        on_device, mesh=mesh, in_specs=in_specs, out_specs=out_specs, check_vma=False
    )
```

```python
import functools
import math

import jax
import jax.numpy as jnp
import numpy as np
from jax import lax
from jax.experimental import pallas as pl
from jax.experimental.pallas import tpu as pltpu
from jax.sharding import PartitionSpec as P

NEG = -1e30
F32 = jnp.float32
BF16 = jnp.bfloat16
VMEM = pl.BlockSpec(memory_space=pltpu.VMEM)
SMEM = pl.BlockSpec(memory_space=pltpu.SMEM)
HBM = pl.BlockSpec(memory_space=pltpu.HBM)


def staged(body, scalars, arrays, late, out_shape, scratch, limit, name, out_specs=None):
    count = len(arrays)

    def kernel(*refs):
        n = len(scalars)
        sources, refs_out = refs[n:n + count], refs[n + count:n + count + len(out_shape)]
        rest = refs[n + count + len(out_shape):]
        held, sems, extra = rest[:count], rest[count], rest[count + 1:]
        copies = [
            pltpu.make_async_copy(src, dst, sems.at[i])
            for i, (src, dst) in enumerate(zip(sources, held))
        ]
        for copy in copies:
            copy.start()
        for copy in copies[:count - late]:
            copy.wait()
        waits = [lambda copy=copy: copy.wait() for copy in copies[count - late:]]
        body(*refs[:n], *held, *waits, *refs_out, *extra)

    return pl.pallas_call(
        kernel,
        in_specs=[SMEM] * len(scalars) + [HBM] * count,
        out_specs=out_specs or [VMEM] * len(out_shape),
        out_shape=out_shape,
        scratch_shapes=[pltpu.VMEM(a.shape, a.dtype) for a in arrays]
        + [pltpu.SemaphoreType.DMA((count,))] + list(scratch),
        compiler_params=pltpu.CompilerParams(vmem_limit_bytes=limit * 2**20),
        name=name,
    )(*scalars, *arrays)


def direct(body, scalars, arrays, out_shape, scratch, limit, name):
    return pl.pallas_call(
        body,
        in_specs=[SMEM] * len(scalars) + [VMEM] * len(arrays),
        out_specs=[VMEM] * len(out_shape),
        out_shape=out_shape,
        scratch_shapes=list(scratch),
        compiler_params=pltpu.CompilerParams(vmem_limit_bytes=limit * 2**20),
        name=name,
    )(*scalars, *arrays)


def swap(a, axis, mask):
    return lax.ppermute(a, axis, [(i, i ^ mask) for i in range(lax.axis_size(axis))])


def reduce_bits(x, axis, order, last=F32):
    first = None
    count = x.shape[0]
    left = list(range(count.bit_length() - 1))[::-1]
    x = x.reshape((2,) * len(left) + x.shape[1:])
    for bit in order:
        dim = left.index(bit)
        left.remove(bit)
        kept = lax.index_in_dim(x, 0, dim, False).astype(F32)
        came = swap(lax.index_in_dim(x, 1, dim, False), axis, 1 << bit)
        x = (kept + came.astype(F32)).astype(BF16 if left else last)
        first = x if first is None else first
    return x, first


def gather_bits(x, axis):
    x = x[None]
    for bit in range(lax.axis_size(axis).bit_length() - 1)[::-1]:
        came = swap(x, axis, 1 << bit)
        x = jnp.stack([x, came], 1).reshape((2 * x.shape[0],) + x.shape[1:])
    return x


def bind(joint, *values):
    return lax.optimization_barrier(values) if joint else values


def trade(pieces, axis, joint=False):
    return [pieces[0], *bind(joint, *(swap(piece, axis, j) for j, piece in enumerate(pieces) if j))]


def reduce_both_ways(nears, fars, axis):
    sums_near, sums_far = [], []
    for near, far in zip(nears, fars):
        came = bind(len(sums_near) > 0, swap(near[1::2], axis, 1), swap(far[2:], axis, 2), *sums_near, *sums_far)
        sums_near.append((near[::2].astype(F32) + came[0].astype(F32)).astype(BF16))
        sums_far.append((far[:2].astype(F32) + came[1].astype(F32)).astype(BF16))
    near, far = jnp.concatenate(sums_near, 1), jnp.concatenate(sums_far, 1)
    more = bind(True, swap(near[1], axis, 2), swap(far[1], axis, 1))
    return near[0].astype(F32) + more[0].astype(F32), far[0].astype(F32) + more[1].astype(F32)


def attention_body(shape, first, *refs):
    first_m, count, rows, together = shape
    if first:
        (scal, table, freq, q_ref, kn_ref, vn_ref, ko_ref, vo_ref, wait_k, wait_v,
         k_out, v_out, q_rot, key_pos, ok_ref, os_ref, inverse, out_sems) = refs
        tokens, head_dim = kn_ref.shape
        pages = table.shape[1]
    else:
        scal, ko_ref, vo_ref, q_rot, key_pos, ok_ref, os_ref = refs
        tokens, head_dim = q_rot.shape[0], ko_ref.shape[2]
    slots, page = ko_ref.shape[0], ko_ref.shape[1]
    heads = q_rot.shape[1] // head_dim
    length, kv_id, blk_id = scal[0], scal[1], scal[2]
    scale = 1.0 / math.sqrt(head_dim)

    if first:
        @pl.loop(0, pages)
        def _(j):
            inverse[table[0, j]] = j

        lane = lax.broadcasted_iota(jnp.int32, (1, page), 1)
        for s in range(slots):
            key_pos[:, s * page:(s + 1) * page] = inverse[blk_id * slots + s] * page + lane

        where_at = (length + lax.broadcasted_iota(jnp.int32, (tokens, head_dim), 0)).astype(F32)
        angle = where_at * freq[...]
        cosine = jnp.cos(angle)
        sine = jnp.sin(angle)
        low = lax.broadcasted_iota(jnp.int32, (tokens, head_dim), 1) < head_dim // 2
        sine = jnp.where(low, -sine, sine)

        def rotate(u):
            u = u.astype(F32)
            return (u * cosine + pltpu.roll(u, head_dim // 2, 1) * sine).astype(BF16)

        for h in range(heads):
            cols = slice(h * head_dim, (h + 1) * head_dim)
            q_rot[:, cols] = rotate(q_ref[:, cols])
        k_rot = rotate(kn_ref[...])

        wait_k()
        wait_v()
        for extra in range(tokens // page + 1):
            logical = length // page + extra
            slot = table[0, jnp.minimum(logical, pages - 1)] - blk_id * slots

            @pl.when((logical < pages) & (slot >= 0) & (slot < slots))
            def _():
                begin = logical * page - length
                at = begin + lax.broadcasted_iota(jnp.int32, (page, tokens), 0)
                pick = (at == lax.broadcasted_iota(jnp.int32, (page, tokens), 1)).astype(BF16)
                fresh_k = jnp.dot(pick, k_rot, preferred_element_type=F32).astype(BF16)
                fresh_v = jnp.dot(pick, vn_ref[...], preferred_element_type=F32).astype(BF16)
                at = begin + lax.broadcasted_iota(jnp.int32, (page, head_dim), 0)
                is_new = (at >= 0) & (at < tokens)
                ko_ref[slot] = jnp.where(is_new, fresh_k, ko_ref[slot])
                vo_ref[slot] = jnp.where(is_new, fresh_v, vo_ref[slot])

        stores = [
            pltpu.make_async_copy(src, dst, out_sems.at[i])
            for i, (src, dst) in enumerate(((ko_ref, k_out), (vo_ref, v_out)))
        ]
        for store in stores:
            store.start()

    keys = ko_ref[...].reshape(slots * page, head_dim)
    values = vo_ref[...].reshape(slots * page, head_dim)
    side_rows = count * rows
    head_rows = 2 * side_rows
    row = lax.broadcasted_iota(jnp.int32, (together * head_rows, 1), 0) % head_rows
    side = row // side_rows
    place = (row % side_rows) // rows + first_m
    token = ((place ^ kv_id) * 2 + (blk_id ^ side)) * rows + row % rows
    lane = lax.broadcasted_iota(jnp.int32, (side_rows, head_dim), 1)
    stats = [jnp.zeros((side_rows, head_dim), F32)] * 2
    for pair in range(heads // together):
        parts = []
        for h in range(pair * together, (pair + 1) * together):
            cols = slice(h * head_dim, (h + 1) * head_dim)
            for s in range(2):
                for m in range(first_m, first_m + count):
                    start = ((kv_id ^ m) * 2 + (blk_id ^ s)) * rows
                    parts.append(q_rot[pl.ds(pl.multiple_of(start, rows), rows), cols])
        queries = jnp.concatenate(parts, 0)
        scores = lax.dot_general(queries, keys, (((1,), (1,)), ((), ())), preferred_element_type=F32)
        masked = jnp.where(key_pos[...] <= length + token, scores, NEG)
        top = jnp.maximum(jnp.max(masked, 1, keepdims=True), 0.1 * NEG)
        weights = jnp.exp2((masked - top) * (scale * math.log2(math.e))).astype(BF16)
        total = jnp.sum(weights.astype(F32), 1, keepdims=True)
        out = jnp.dot(weights, values, preferred_element_type=F32)
        some = total > 0.0
        safe = jnp.where(some, total, 1.0)
        out = (out / safe).astype(BF16)
        log_sum = jnp.where(some, top * scale + jnp.log(safe), NEG)
        for i in range(together):
            h = pair * together + i
            cols = slice(h * head_dim, (h + 1) * head_dim)
            for s, out_ref in enumerate((ok_ref, os_ref)):
                at = i * head_rows + s * side_rows
                out_ref[:, cols] = out[at:at + side_rows]
                here = (lane % heads == h) & (lane < 3 * heads)
                stats[s] = jnp.where(here, log_sum[at:at + side_rows], stats[s])
    for stat, out_ref in zip(stats, (ok_ref, os_ref)):
        one = stat.astype(BF16).astype(F32)
        two = (stat - one).astype(BF16).astype(F32)
        stat = jnp.where(lane < heads, one, jnp.where(lane < 2 * heads, two, stat - one - two))
        out_ref[:, heads * head_dim:] = stat.astype(BF16)
    if first:
        for store in stores:
            store.wait()


def attend_first(scal, table, q, k_new, v_new, k_cache, v_cache, rows, first_m, count):
    tokens, head_dim = k_new.shape
    width = q.shape[1]
    slots, page = k_cache.shape[0], k_cache.shape[1]
    side = count * rows
    pair = np.arange(head_dim) % (head_dim // 2)
    freq = jnp.asarray((1e6 ** (-2.0 * pair / head_dim)).astype(np.float32)[None])
    return staged(
        functools.partial(attention_body, (first_m, count, rows, 4 if count == 1 else 1), True),
        [scal, table], [freq, q, k_new, v_new, k_cache, v_cache], 2,
        [
            jax.ShapeDtypeStruct(k_cache.shape, BF16),
            jax.ShapeDtypeStruct(v_cache.shape, BF16),
            jax.ShapeDtypeStruct((tokens, width), BF16),
            jax.ShapeDtypeStruct((1, slots * page), jnp.int32),
            jax.ShapeDtypeStruct((side, width + head_dim), BF16),
            jax.ShapeDtypeStruct((side, width + head_dim), BF16),
        ],
        [pltpu.SMEM((table.shape[1],), jnp.int32), pltpu.SemaphoreType.DMA((2,))],
        56, "attend_first", [HBM, HBM] + [VMEM] * 4)


def attend_next(scal, keys, values, q_rot, key_pos, rows, first_m, count):
    width, head_dim = q_rot.shape[1], keys.shape[2]
    side = count * rows
    return pl.pallas_call(
        functools.partial(attention_body, (first_m, count, rows, 1), False),
        in_specs=[SMEM] + [VMEM] * 4,
        out_specs=[VMEM] * 2,
        out_shape=[jax.ShapeDtypeStruct((side, width + head_dim), BF16)] * 2,
        compiler_params=pltpu.CompilerParams(vmem_limit_bytes=40 * 2**20),
        cost_estimate=pl.CostEstimate(flops=8 * 10**9, bytes_accessed=10**6, transcendentals=0),
        name="attend_next",
    )(scal, keys, values, q_rot, key_pos)


def project_body(head_dim, scal, o1, o2, wa, wb, *rest):
    outs, attn = rest[:-1], rest[-1]
    width = attn.shape[1]
    heads = width // head_dim
    depth, model = wa.shape
    blk_id = scal[2]
    rows = outs[0].shape[0]
    logs = []
    for o in (o1, o2):
        stat = o[:, width:].astype(F32)
        logs.append([sum(stat[:, h + i * heads:h + i * heads + 1] for i in range(3)) for h in range(heads)])
    for h in range(heads):
        cols = slice(h * head_dim, (h + 1) * head_dim)
        first, second = logs[0][h], logs[1][h]
        top = jnp.maximum(first, second)
        f1, f2 = jnp.exp(first - top), jnp.exp(second - top)
        mixed = f1 * o1[:, cols].astype(F32) + f2 * o2[:, cols].astype(F32)
        attn[:, cols] = (mixed / (f1 + f2)).astype(BF16)
    mine = attn[:, pl.ds(pl.multiple_of(blk_id * depth, depth), depth)]
    other = attn[:, pl.ds(pl.multiple_of((1 - blk_id) * depth, depth), depth)]
    step = model // 4
    for n in range(0, model, step):
        out = (
            jnp.dot(mine, wa[:, n:n + step], preferred_element_type=F32)
            + jnp.dot(other, wb[:, n:n + step], preferred_element_type=F32)
        ).astype(BF16)
        for i, out_ref in enumerate(outs):
            out_ref[:, n:n + step] = out[i * rows:(i + 1) * rows]


def project(scal, o1, o2, wa, wb, head_dim, count):
    rows = o1.shape[0]
    width = o1.shape[1] - head_dim
    return direct(
        functools.partial(project_body, head_dim), [scal], [o1, o2, wa, wb],
        [jax.ShapeDtypeStruct((rows // count, wa.shape[1]), BF16)] * count,
        [pltpu.VMEM((rows, width), BF16)], 32, "project")


def norm_body(scal, x_ref, gain_ref, *rest):
    terms, resid_ref, pieces, held = rest[:3], rest[3], rest[4:-1], rest[-1]
    part = pieces[0].shape[1]
    resid = x_ref[...].astype(F32)
    for term in terms:
        resid = resid + term[...].astype(F32)
    resid_ref[...] = resid
    scale = lax.rsqrt(jnp.mean(resid * resid, axis=-1, keepdims=True) + 1e-05)
    held[...] = (resid * scale * gain_ref[...].astype(F32)).astype(BF16)
    for j, piece in enumerate(pieces):
        start = pl.multiple_of((scal[3] ^ j) * part, part)
        piece[...] = held[:, pl.ds(start, part)]


def norm_cut(scal, x, terms, gain, reqs):
    rows, model = terms[0].shape
    part = model // reqs
    return direct(
        norm_body, [scal], [x, gain, *terms],
        [jax.ShapeDtypeStruct((rows, model), F32)]
        + [jax.ShapeDtypeStruct((rows, part), BF16)] * reqs,
        [pltpu.VMEM((rows, model), BF16)], 8, "norm_cut")


def partial_gate_up(feds, weights):
    flat = jnp.concatenate(feds, 0)
    flat = flat.reshape(-1, flat.shape[-1])
    both = jnp.concatenate(
        [jnp.dot(flat, w, preferred_element_type=F32).astype(BF16) for w in weights], 1)
    reqs, rows = feds[0].shape[:2]
    return both.reshape(len(feds), reqs, rows, -1).transpose(1, 0, 2, 3)


def down(hiddens, weights, groups):
    hidden = jnp.concatenate(hiddens, 0)
    depth = weights[0].shape[0]
    out = (
        jnp.dot(hidden[:, :depth], weights[0], preferred_element_type=F32)
        + jnp.dot(hidden[:, depth:], weights[1], preferred_element_type=F32)
    ).astype(BF16)
    out = out.reshape(len(hiddens), groups, -1, out.shape[1])
    return [out[:, m].reshape(-1, out.shape[-1]) for m in range(groups)]


def finish_body(chunks, scal, *refs):
    out_ref = refs[-1]
    for c in range(chunks):
        resid, own_a, own_b, own_c, back_x, back_y = refs[6 * c:6 * c + 6]
        rows, half = back_x.shape[0], back_x.shape[1] // 2
        here = slice(c * rows, (c + 1) * rows)
        whole = own_a[...].astype(F32) + own_b[...].astype(F32) + own_c[...].astype(F32)
        for block, side, value in (
            (0, 0, whole[:, :half]), (0, 1, whole[:, half:2 * half]),
            (1, 0, whole[:, 2 * half:3 * half]), (2, 1, whole[:, 3 * half:]),
            (1, 1, back_x[:, :half]), (3, 1, back_x[:, half:]),
            (2, 0, back_y[:, :half]), (3, 0, back_y[:, half:]),
        ):
            start = (scal[3] ^ block) * (2 * half) + side * half
            cols = pl.ds(pl.multiple_of(start, half), half)
            out_ref[here, cols] = (resid[:, cols] + value.astype(F32)).astype(BF16)


def finish(scal, parts):
    rows, model = parts[0][0].shape
    return direct(
        functools.partial(finish_body, len(parts)), [scal], [a for part in parts for a in part],
        [jax.ShapeDtypeStruct((len(parts) * rows, model), BF16)], [], 8, "finish")[0]


def after(a, *others):
    return lax.optimization_barrier((a,) + others)[0]


def hidden_of(both):
    gate, up = jnp.split(both, 2, -1)
    return (jax.nn.silu(gate) * up).astype(BF16)


def reduce_four(x, axis, joint=False):
    came = swap(x[3], axis, 1)
    both = (x[2].astype(F32) + came.astype(F32)).astype(BF16)
    return [x[0], *bind(joint, swap(x[1], axis, 1), swap(both, axis, 2))], both


def halve_four(x, axis, joint=False):
    came = swap(jnp.stack([x[1], x[3]]), axis, 1)
    both = (x[2].astype(F32) + came[1].astype(F32)).astype(BF16)
    return [x[0], came[0], swap(both, axis, 2)], both


def total(terms):
    return terms[0].astype(F32) + terms[1].astype(F32) + terms[2].astype(F32)


def product(rows, weights):
    depth = weights[0][0].shape[0]
    near, far = rows[:, :depth], rows[:, depth:]
    return jnp.concatenate([
        (
            jnp.dot(near, pair[0], preferred_element_type=F32)
            + jnp.dot(far, pair[1], preferred_element_type=F32)
        ).astype(BF16)
        for pair in weights
    ], 1)


def on_device(x_resid, q_new, k_new, v_new, k_cache, v_cache, cache_len, page_table,
              wo, norm_gain, w_gate, w_up, w_down):
    reqs, kvs = lax.axis_size("req"), lax.axis_size("kv")
    rows, model = x_resid.shape[1:]
    head_dim = k_new.shape[2]
    scal = jnp.stack(
        [cache_len[0], lax.axis_index("kv"), lax.axis_index("blk"), lax.axis_index("req")]
    ).astype(jnp.int32)
    wo_far = swap(wo, "blk", 1)
    fast = reqs == 4 and kvs == 4
    half = model // reqs // 2
    cuts = [w_down[:, :half], w_down[:, half:]]
    first_m = kvs - 1 if fast else 0
    keys_out, values_out, q_rot, key_pos, o_keep, o_send = attend_first(
        scal, page_table, q_new[0], k_new[0], v_new[0], k_cache[0, 0], v_cache[0, 0],
        rows, first_m, kvs - first_m)
    projected = project(scal, o_keep, swap(o_send, "blk", 1), wo, wo_far, head_dim, kvs - first_m)
    if first_m:
        o_keep, o_send = attend_next(
            scal, keys_out, values_out, after(q_rot, projected[0], *cuts), key_pos, rows, 0, first_m)
        o_came = swap(o_send, "blk", 1)
        projected = [*project(scal, o_keep, o_came, wo, wo_far, head_dim, first_m), *projected]
    projected = [list(projected)]
    layer = four_way if fast else any_way
    layer_out = layer(x_resid[0], projected, scal, norm_gain[None], w_gate, w_up, cuts if fast else w_down, reqs, kvs)
    return layer_out[None], keys_out[None, None], values_out[None, None]


def any_way(x_resid, projected, scal, gain, w_gate, w_up, w_down, reqs, kvs):
    rows, model = x_resid.shape
    part = model // reqs
    req_order = list(range(reqs.bit_length() - 1))
    kv_order = list(range(kvs.bit_length() - 1))
    gate_far, up_far, down_far = (swap(w, "blk", 1) for w in (w_gate, w_up, w_down))
    summed, _ = reduce_bits(jnp.stack(projected[0]), "kv", kv_order)
    resid = x_resid.astype(F32) + summed
    scale = lax.rsqrt(jnp.mean(resid * resid, axis=-1, keepdims=True) + 1e-05)
    cut = (resid * scale * gain.astype(F32)).astype(BF16).reshape(rows, reqs, part)
    pieces = [lax.dynamic_index_in_dim(cut, scal[3] ^ j, 1, False) for j in range(reqs)]
    fed = gather_bits(jnp.stack(trade(pieces, "req")), "kv")
    flat = fed.reshape(kvs * reqs * rows, part)
    hidden = []
    for gate_w, up_w in ((w_gate, w_up), (gate_far, up_far)):
        both = jnp.concatenate(
            [jnp.dot(flat, w, preferred_element_type=F32).astype(BF16) for w in (gate_w, up_w)], 1)
        both = both.reshape(kvs, reqs, rows, -1).transpose(1, 0, 2, 3)
        both, _ = reduce_bits(both, "req", req_order)
        every = jnp.stack(trade([hidden_of(both)] * reqs, "req"))
        hidden.append(every.reshape(reqs * kvs * rows, -1))
    out = (
        jnp.dot(hidden[0], w_down, preferred_element_type=F32)
        + jnp.dot(hidden[1], down_far, preferred_element_type=F32)
    ).astype(BF16)
    out = out.reshape(reqs, kvs, rows, part).transpose(1, 0, 2, 3)
    out, _ = reduce_bits(out, "kv", kv_order, BF16)
    came = jnp.stack(trade([out[j] for j in range(reqs)], "req"))
    mlp = [lax.dynamic_index_in_dim(came, scal[3] ^ j, 0, False) for j in range(reqs)]
    return (resid + jnp.concatenate(mlp, 1).astype(F32)).astype(BF16)


def four_way(x_resid, projected, scal, gain, w_gate, w_up, cuts, reqs, kvs):
    step, model = projected[0][0].shape
    part = model // reqs
    half = part // 2
    lent = [swap(cut, "req", mask) for cut, mask in zip(cuts, (1, 2))]
    summed, boths = [], []
    for sums in projected:
        if boths:
            sums[3] = after(sums[3], boths[-1])
        terms, both = reduce_four(sums, "kv", False)
        summed.append(terms)
        boths.append(both)

    resids, fed = [], []
    held = None
    for c, terms in enumerate(summed):
        if held is not None:
            terms[0] = after(terms[0], *held)
        resid, *pieces = norm_cut(scal, x_resid[c * step:(c + 1) * step], terms, gain, reqs)
        resids.append(resid)
        pieces[-1] = after(pieces[-1], *lent)
        got = jnp.stack(trade(pieces, "req", True))
        two, one = bind(True, swap(got, "kv", 2), swap(got, "kv", 1))
        three = swap(two, "kv", 1)
        fed.append([got, one, two, three])
        held = [one, two]
        gated = [two]

    gate_far, up_far = (swap(w, "blk", 1) for w in (w_gate, w_up))
    weights = [(w, swap(w, "blk", 1)) for w in (*cuts, *lent)]

    hiddens = []
    for got, one, two, three in fed:
        nears = [partial_gate_up([got, one, two], (w_gate, w_up))]
        fars = [partial_gate_up([got, one, two], (gate_far, up_far))]
        three = after(three, nears[0], fars[0])
        nears.append(partial_gate_up([three], (w_gate, w_up)))
        fars.append(partial_gate_up([three], (gate_far, up_far)))
        near, far = reduce_both_ways(nears, fars, "req")
        hidden = jnp.concatenate([hidden_of(near), hidden_of(far)], -1).reshape(kvs * step, -1)
        hiddens.append(hidden)

    owns, rests, parts = [], [], []
    for c, hidden in enumerate(hiddens):
        from_y, from_x = bind(True, swap(hidden, "req", 2), swap(hidden, "req", 1))
        first, second, over_x, over_y = weights
        own, both = reduce_four(product(hidden, weights).reshape(kvs, step, -1), "kv", False)
        from_y = after(from_y, both)
        rest = jnp.concatenate([product(from_y, (first, over_x)), product(from_x, (second, over_y))], 1)
        rest = list(rest.reshape(kvs, step, -1))
        rest[3] = after(rest[3], *own)
        rest, _ = reduce_four(rest, "kv", False)
        rest = total(rest).astype(BF16)
        rests.append(rest)
        back_y, back_x = bind(True, swap(rest[:, :part], "req", 2), swap(rest[:, part:], "req", 1))
        parts.append([resids[c], *own, back_x, back_y])
    return finish(scal, parts)


def solution(mesh):
    in_specs = (
        P("req", ("kv", "blk"), None),
        P("req", None, "kv"),
        P("req", None, "kv"),
        P("req", None, "kv"),
        P("req", "kv", "blk", None, None),
        P("req", "kv", "blk", None, None),
        P("req"),
        P("req", None),
        P(("kv", "blk"), None),
        P(),
        P("req", ("kv", "blk")),
        P("req", ("kv", "blk")),
        P(("kv", "blk"), "req"),
    )
    out_specs = (
        P("req", ("kv", "blk"), None),
        P("req", "kv", "blk", None, None),
        P("req", "kv", "blk", None, None),
    )
    return jax.shard_map(
        on_device, mesh=mesh, in_specs=in_specs, out_specs=out_specs, check_vma=False
    )
```
